256 devices in a mesh: dp: 8 (over x, y_lo), space: 32 (over y_hi, z, core).
Axes of the slice: x: 4, y: 4 (y_hi: 2, y_lo: 2; y = y_hi * 2 + y_lo), z: 8, core: 2. Of those that a mesh axis runs over, the one named last changes fastest.
Arguments:
- volumes: bfloat16 [128, 4, 128, 4, 512], P('dp', None, 'space'), may hold values from -6 to 6
- targets: float32 [128, 4], P('dp'), may hold values from -6 to 6
- counts: int32 [32], replicated, may hold values from 0 to 2, as said below
- w_conv1: bfloat16 [3, 3, 3, 32, 4], replicated, may hold values from -0.625 to 0.625
- w_conv2: bfloat16 [3, 3, 3, 64, 32], replicated, may hold values from -0.21875 to 0.21875
- w_dense1: bfloat16 [2048, 128], replicated, may hold values from -1.5 to 1.5
- w_dense2: bfloat16 [128, 64], replicated, may hold values from -0.5 to 0.5
- w_dense3: bfloat16 [64, 4], replicated, may hold values from -0.75 to 0.75
Outputs:
- loss: float32 [], replicated
- grad_w1: float32 [3, 3, 3, 32, 4], replicated
- grad_w2: float32 [3, 3, 3, 64, 32], replicated
- grad_d1: float32 [2048, 128], replicated
- grad_d2: float32 [128, 64], replicated
- grad_d3: float32 [64, 4], replicated
The draws below stay inside these ranges and needn't reach their ends.
Inputs may be any that keep to these rules, and one draw needn't show every extreme that they name: The counts sum to 16; a group may hold no sample, and the largest holds exactly 2.
All inputs are finite; a program needn't handle non-finite values.
Results may differ from the reference program's by a relative error of at most 0.018.
Values may be sent and summed in bfloat16 or wider, within the bound.
No kernel may reach another device: no remote copies, remote signals or barrier semaphores. Data moves between devices by JAX's collectives and lax.ppermute only.
A program may use at most 128 MiB of HBM per device.

```python
import jax
import jax.numpy as jnp
from jax import lax

CIN = 4
C1 = 32
C2 = 64
H1 = 128
H2 = 64
NOUT = 4
NY = 4
NZ = 512
MOST = 2
BATCH = 16
SAMPLES = 128
NX = 128
F = 2048
N_DP = 8
N_SPACE = 32


def draw_counts(key, part):
    key = jax.random.fold_in(key, 7)
    slots = N_SPACE * MOST
    order = jax.random.permutation(key, slots).astype(jnp.int32)
    chosen = jax.random.randint(jax.random.fold_in(key, 1), (), 0, N_SPACE).astype(jnp.int32)
    owner = jnp.arange(slots, dtype=jnp.int32) // MOST
    scores = jnp.where(owner == chosen, order - slots, order).astype(jnp.int32)
    ranking = jnp.argsort(jnp.argsort(scores))
    picked = (ranking < BATCH).astype(jnp.int32)
    return jnp.sum(picked.reshape(N_SPACE, MOST), axis=1).astype(jnp.int32)


def block_scale(rng, dims, shards, low, top_value):
    def one(position, parts):
        draws = jax.random.uniform(jax.random.fold_in(jax.random.fold_in(rng, 6), position), (parts,), jnp.float32, low / len(shards), top_value / len(shards))
        return jnp.repeat(jnp.exp(draws), dims[position] // parts).reshape((-1,) + (1,) * (len(dims) - position - 1))

    gain = one(*shards[0])
    for cut in shards[1:]:
        gain = gain * one(*cut)
    return gain


def scatter_about(stream_key, extent, width, most, split=(), held_as=jnp.bfloat16):
    values = width * jax.random.normal(stream_key, extent, jnp.float32)
    if split:
        values = values * block_scale(stream_key, extent, split, -0.22, 0.18)
    return jnp.clip(values, -most, most).astype(held_as)


def setup_inputs(seed: int = 0) -> dict:
    streams_of = jax.random.split(jax.random.key(seed), 9)
    volumes = scatter_about(streams_of[0], (SAMPLES, CIN, NX, NY, NZ), 1.0, 6.0, ((0, 8), (2, 32)))
    targets = scatter_about(streams_of[1], (SAMPLES, NOUT), 1.0, 6.0, ((0, 8),), jnp.float32)
    counts = draw_counts(jax.random.fold_in(streams_of[8], 71), 0)
    w_conv1 = scatter_about(streams_of[3], (3, 3, 3, C1, CIN), (27 * CIN) ** -0.5, 0.625)
    w_conv2 = scatter_about(streams_of[4], (3, 3, 3, C2, C1), (27 * C1) ** -0.5, 0.21875)
    w_dense1 = scatter_about(streams_of[5], (F, H1), (F // 128) ** -0.5, 1.5)
    w_dense2 = scatter_about(streams_of[6], (H1, H2), H1 ** -0.5, 0.5)
    w_dense3 = scatter_about(streams_of[7], (H2, NOUT), H2 ** -0.5, 0.75)
    return dict(volumes=volumes, targets=targets, counts=counts, w_conv1=w_conv1, w_conv2=w_conv2, w_dense1=w_dense1, w_dense2=w_dense2, w_dense3=w_dense3)


def leaky_relu(values):
    return values * (0.65 + 0.35 * jnp.tanh(values))

def slope_of(values):
    tangent = jnp.tanh(values)
    return 0.65 + 0.35 * tangent + 0.35 * values * (1.0 - tangent * tangent)

def conv_down(field, weight):
    kernel = jnp.transpose(weight.astype(jnp.float32), (3, 4, 0, 1, 2))
    result = lax.conv_general_dilated(field[None], kernel, (2, 2, 2), ((1, 0), (1, 0), (1, 0)), dimension_numbers=('NCDHW', 'OIDHW', 'NCDHW'), precision=lax.Precision.HIGHEST)
    return result[0]

def forward_volume(volume, w_conv1, w_conv2):
    hidden1 = conv_down(volume.astype(jnp.float32), w_conv1)
    act1 = leaky_relu(hidden1).astype(jnp.bfloat16)
    hidden2 = conv_down(act1.astype(jnp.float32), w_conv2)
    act2 = leaky_relu(hidden2).astype(jnp.bfloat16)
    return (hidden1, act1, hidden2, act2)

def reference(volumes, targets, counts, w_conv1, w_conv2, w_dense1, w_dense2, w_dense3):

    def feature_step(carry, volume):
        hidden1, act1, hidden2, act2 = forward_volume(volume, w_conv1, w_conv2)
        pooled = lax.optimization_barrier(jnp.mean(act2.astype(jnp.float32), axis=3)).reshape(-1).astype(jnp.bfloat16)
        return (carry, pooled)
    unused, feats = lax.scan(feature_step, jnp.zeros((), jnp.float32), volumes)
    ends = jnp.cumsum(counts, dtype=jnp.int32)
    local_ids = jnp.arange(BATCH, dtype=jnp.int32)
    owners = lax.optimization_barrier(jnp.sum((ends[None, :] <= local_ids[:, None]).astype(jnp.int32), axis=1)).astype(jnp.int32)
    replica = jnp.arange(SAMPLES, dtype=jnp.int32) // BATCH
    groups = replica * N_SPACE + jnp.tile(owners, N_DP)
    onehot = (groups[:, None] == jnp.arange(N_DP * N_SPACE, dtype=jnp.int32)[None, :]).astype(jnp.float32)
    group_sizes = jnp.maximum(jnp.tile(counts, N_DP), 1).astype(jnp.float32)

    def group_mean(values):
        sums = jnp.dot(onehot.T, values, precision=lax.Precision.HIGHEST)
        return jnp.dot(onehot, sums / group_sizes[:, None], precision=lax.Precision.HIGHEST)
    dense1 = jnp.dot(feats, w_dense1, preferred_element_type=jnp.float32)
    centred = dense1 - 0.5 * group_mean(dense1)
    out1 = leaky_relu(centred).astype(jnp.bfloat16)
    dense2 = jnp.dot(out1, w_dense2, preferred_element_type=jnp.float32)
    out2 = leaky_relu(dense2).astype(jnp.bfloat16)
    pred = jnp.dot(out2, w_dense3, preferred_element_type=jnp.float32)
    diff = pred - targets
    loss = 0.5 * jnp.sum(diff * diff) / BATCH
    gpred = (diff / BATCH).astype(jnp.bfloat16)
    grad_d3 = jnp.dot(out2.T, gpred, preferred_element_type=jnp.float32)
    gdense2 = (jnp.dot(gpred, w_dense3.T, preferred_element_type=jnp.float32) * slope_of(dense2)).astype(jnp.bfloat16)
    grad_d2 = jnp.dot(out1.T, gdense2, preferred_element_type=jnp.float32)
    gcentred = jnp.dot(gdense2, w_dense2.T, preferred_element_type=jnp.float32) * slope_of(centred)
    gdense1 = (gcentred - 0.5 * group_mean(gcentred)).astype(jnp.bfloat16)
    grad_d1 = jnp.dot(feats.T, gdense1, preferred_element_type=jnp.float32)
    gfeats = jnp.dot(gdense1, w_dense1.T, preferred_element_type=jnp.float32).astype(jnp.bfloat16)

    def grad_step(carry, pair):
        volume, gfeat = pair
        hidden1, act1, hidden2, act2 = forward_volume(volume, w_conv1, w_conv2)
        spread = gfeat.reshape(C2, NX // 4, NY // 4)[..., None].astype(jnp.float32) / (NZ // 4)
        ghidden2 = (spread * slope_of(hidden2)).astype(jnp.bfloat16)
        unused_a, back_two = jax.vjp(conv_down, act1.astype(jnp.float32), w_conv2.astype(jnp.float32))
        gact1, step_w2 = back_two(ghidden2.astype(jnp.float32))
        ghidden1 = (gact1 * slope_of(hidden1)).astype(jnp.bfloat16)
        unused_b, back_one = jax.vjp(lambda kernel: conv_down(volume.astype(jnp.float32), kernel), w_conv1.astype(jnp.float32))
        step_w1, = back_one(ghidden1.astype(jnp.float32))
        return ((carry[0] + step_w1, carry[1] + step_w2), None)
    start = (jnp.zeros((3, 3, 3, C1, CIN), jnp.float32), jnp.zeros((3, 3, 3, C2, C1), jnp.float32))
    (grad_w1, grad_w2), unused_c = lax.scan(grad_step, start, (volumes, gfeats))
    return (loss, grad_w1, grad_w2, grad_d1, grad_d2, grad_d3)
```

```python
import functools

import jax
import jax.numpy as jnp
import numpy as np
from jax import lax
from jax.experimental import pallas as pl
from jax.experimental.pallas import tpu as pltpu
from jax.sharding import Mesh
from jax.sharding import PartitionSpec as P

BF = jnp.bfloat16
F32 = jnp.float32
SLABS = ("yh", "z", "core")
PLANE = ("x", "yl", "yh")
S = 16
LANES = 128
WIDE = S * LANES
HALF = 176
CHUNK = 512

NN = (((1,), (0,)), ((), ()))
NT = (((1,), (1,)), ((), ()))
TN = (((0,), (0,)), ((), ()))


def mm(a, b, dims=NN):
    return lax.dot_general(a, b, dims, preferred_element_type=F32)


def mm_exact(a, b):
    return lax.dot_general(
        a, b, NN, preferred_element_type=F32, precision=lax.Precision.HIGHEST
    )


def leaky(v, t):
    return v * (0.65 + 0.35 * t)


def slope(v, t):
    return 0.65 + 0.35 * t + 0.35 * v * (1.0 - t * t)


def split_matrix():
    m = np.zeros((512, 640), np.float32)
    for k, offset in enumerate((-1, 0, 1, 2, 3)):
        for i in range(128):
            if 4 * i + offset >= 0:
                m[4 * i + offset, k * 128 + i] = 1.0
    return m


def band_matrices():
    own = np.zeros((2, 2, 128, 192), np.float32)
    rim = np.zeros((2, 128, 48), np.float32)
    for i in range(2):
        for j in range(2):
            for a in range(3):
                for b in range(3):
                    x, y = 2 * i + a - 1, 2 * j + b - 1
                    if y < 0:
                        continue
                    for e in range(3):
                        for c in range(4):
                            src = ((a * 3 + b) * 3 + e) * 4 + c
                            if x >= 0:
                                own[i, j, src, ((e * 4 + c) * 4 + x) * 4 + y] = 1.0
                            else:
                                rim[j, src, (e * 4 + c) * 4 + y] = 1.0
    return own, rim


def lane_ids(shape):
    return lax.broadcasted_iota(jnp.int32, shape, len(shape) - 1)


def shift_up(x):
    parts = []
    for k in range(x.shape[1] // LANES):
        p = pltpu.roll(x[:, k * LANES : (k + 1) * LANES], 1, 1)
        parts.append(jnp.where(lane_ids(p.shape) == 0, 0.0, p))
    return jnp.concatenate(parts, axis=1)


def shift_down(x):
    parts = []
    for k in range(x.shape[1] // LANES):
        p = pltpu.roll(x[:, k * LANES : (k + 1) * LANES], LANES - 1, 1)
        parts.append(jnp.where(lane_ids(p.shape) == LANES - 1, 0.0, p))
    return jnp.concatenate(parts, axis=1)


def store_plane(h, s, cols, a1_ref, slope_ref):
    t = jnp.tanh(h)
    act = leaky(h, t)
    slope_ref[s, :, cols] = slope(h, t).astype(BF)
    if s == 0:
        a1_ref[64:128, cols] = act.astype(BF)
    else:
        a1_ref[128:192, cols] = act.astype(BF)
        a1_ref[0:64, cols] = shift_up(act).astype(BF)


def first_kernel(v_ref, split_ref, w1_ref, own_ref, w2_ref, x4_ref, a1_ref, slope_ref, send_ref):
    w = jnp.concatenate(
        [mm(w1_ref[...], own_ref[1, j]).astype(BF) for j in range(2)], axis=0
    )
    for q in range(4):
        d = mm(v_ref[q * 256 : (q + 1) * 256, :], split_ref[...])
        for k in range(5):
            for n in range(4):
                x4_ref[k * 64 : (k + 1) * 64, (4 * q + n) * LANES : (4 * q + n + 1) * LANES] = d[
                    n * 64 : (n + 1) * 64, k * LANES : (k + 1) * LANES
                ].astype(BF)
    for q in range(4):
        cols = slice(q * CHUNK, (q + 1) * CHUNK)
        for s in range(2):
            h = mm(w, x4_ref[s * 128 : s * 128 + 192, cols])
            store_plane(h, s, cols, a1_ref, slope_ref)
        send_ref[:, cols] = mm(w2_ref[0], a1_ref[:, cols]).astype(BF)


def second_kernel(
    halo_ref, split_ref, w1_ref, own_ref, rim_ref, w2_ref, x4_ref, a1b_ref, part_ref,
    xh_ref, a1_ref, slope_ref, slope2_ref, pay_ref, fown_ref,
):
    w = jnp.concatenate(
        [mm(w1_ref[...], own_ref[0, j]).astype(BF) for j in range(2)], axis=0
    )
    wh = jnp.concatenate([mm(w1_ref[...], rim_ref[j]).astype(BF) for j in range(2)], axis=0)
    d = mm(halo_ref[...], split_ref[...])
    for k in range(5):
        for n in range(S):
            xh_ref[k * 16 : (k + 1) * 16, n * LANES : (n + 1) * LANES] = d[
                n * 16 : (n + 1) * 16, k * LANES : (k + 1) * LANES
            ].astype(BF)
    total = jnp.zeros((S, 64), F32)
    for q in range(4):
        cols = slice(q * CHUNK, (q + 1) * CHUNK)
        for s in range(2):
            h = mm(w, x4_ref[s * 128 : s * 128 + 192, cols]) + mm(
                wh, xh_ref[s * 32 : s * 32 + 48, cols]
            )
            store_plane(h, s, cols, a1_ref, slope_ref)
        h2 = mm(w2_ref[1], a1_ref[:, cols]) + mm(w2_ref[2], a1b_ref[:, cols])
        h2 = h2 + part_ref[:, cols].astype(F32)
        t = jnp.tanh(h2)
        act2 = leaky(h2, t).astype(BF)
        slope2_ref[:, cols] = slope(h2, t).astype(BF)
        rows = lax.broadcasted_iota(jnp.int32, (S, CHUNK), 0)
        owner = lax.shift_right_logical(lane_ids((S, CHUNK)), 7) + 4 * q
        pick = jnp.where(rows == owner, 1.0, 0.0).astype(BF)
        total = total + mm(pick, act2, NT)
    feats = total * (1.0 / 128.0)
    pay_ref[...] = jnp.concatenate([feats[0:8], feats[8:16]], axis=1).astype(BF)
    fown_ref[...] = jnp.concatenate([feats, jnp.zeros((S, 64), F32)], axis=1).astype(BF)


def tail_kernel(
    g_ref, fown_ref, w1_ref, w1own_ref, w2_ref, w3_ref, same_ref, target_ref, pay_ref, gf_ref
):
    low = lane_ids((8, LANES)) < 64
    pairs = []
    for p in range(16):
        ga, gb = g_ref[2 * p].astype(F32), g_ref[2 * p + 1].astype(F32)
        lo = jnp.where(low, ga, pltpu.roll(gb, 64, 1))
        hi = jnp.where(low, pltpu.roll(ga, 64, 1), gb)
        pairs.append(jnp.concatenate([lo, hi], axis=0).astype(BF))
    feats = jnp.concatenate(pairs, axis=1)
    same = same_ref[...]
    dense1 = mm(feats, w1_ref[...])
    centred = dense1 - 0.5 * mm_exact(same, dense1)
    t1 = jnp.tanh(centred)
    out1 = leaky(centred, t1).astype(BF)
    dense2 = mm(out1, w2_ref[...])
    t2 = jnp.tanh(dense2)
    out2 = leaky(dense2, t2).astype(BF)
    diff = mm(out2, w3_ref[...]) - target_ref[...]
    loss = jnp.sum(jnp.sum(diff * diff, axis=1, keepdims=True), axis=0, keepdims=True) / 32.0
    gpred = (diff / 16.0).astype(BF)
    gdense2 = (mm(gpred, w3_ref[...], NT) * slope(dense2, t2)).astype(BF)
    gcentred = mm(gdense2, w2_ref[...], NT) * slope(centred, t1)
    gdense1 = (gcentred - 0.5 * mm_exact(same, gcentred)).astype(BF)
    gf_ref[...] = mm(w1own_ref[...], gdense1, NT)
    lanes = lane_ids((S, LANES))
    top = lax.broadcasted_iota(jnp.int32, (S, LANES), 0) == 0
    high = loss.astype(BF).astype(F32)
    mid = (loss - high).astype(BF).astype(F32)
    rest = loss - high - mid
    last = fown_ref[...].astype(F32) + gpred.astype(F32)
    for k, piece in enumerate((high, mid, rest)):
        last = last + jnp.where(jnp.logical_and(top, lanes == 68 + k), piece, 0.0)
    pay_ref[0:16] = out1
    pay_ref[16:32] = gdense1
    pay_ref[32:48] = (out2.astype(F32) + pltpu.roll(gdense2.astype(F32), 64, 1)).astype(BF)
    pay_ref[48:64] = last.astype(BF)


def back_kernel(
    core_ref, gf_ref, slope2_ref, next2_ref, block_ref, s1a_ref, s1b_ref, a1a_ref, a1b_ref,
    x4_ref, xh_ref, own_ref, rim_ref, keep_ref, send_ref, g_ref, h_ref, w_ref,
):
    gf = gf_ref[...].astype(BF).astype(F32) * (1.0 / 128.0)
    for q in range(4):
        cols = slice(q * CHUNK, (q + 1) * CHUNK)
        spread = jnp.concatenate(
            [
                jnp.broadcast_to(gf[:, 4 * q + n : 4 * q + n + 1], (128, LANES))
                for n in range(4)
            ],
            axis=1,
        )
        go = spread[0:64] * slope2_ref[:, cols].astype(F32)
        gn = spread[64:128] * next2_ref[:, cols].astype(F32)
        g_ref[0:64, cols] = go.astype(BF)
        g_ref[64:128, cols] = gn.astype(BF)
        g_ref[128:192, cols] = shift_down(go).astype(BF)
        g_ref[192:256, cols] = shift_down(gn).astype(BF)
        gact = mm(block_ref[...], g_ref[:, cols])
        for s in range(2):
            for i, ref in enumerate((s1a_ref, s1b_ref)):
                r = (2 * s + i) * 64
                h_ref[s, i * 64 : (i + 1) * 64, cols] = (
                    gact[r : r + 64] * ref[s, :, cols].astype(F32)
                ).astype(BF)
    go, gn = g_ref[0:64, :], g_ref[64:128, :]
    a1 = mm(go, a1a_ref[...], NT)
    a2 = mm(go, a1b_ref[...], NT)
    a0 = mm(gn, a1b_ref[...], NT)
    w_ref[0:64] = a1[:, :128]
    w_ref[64:128] = a2[:, :128]
    w_ref[128:192] = a0[:, :128]
    w_ref[192:256] = jnp.concatenate([a1[:, 128:192], a2[:, 128:192]], axis=1)
    w_ref[256:320] = jnp.concatenate([a0[:, 128:192], jnp.zeros((64, 64), F32)], axis=1)
    r = mm(h_ref[0], x4_ref[0:192, :], NT) + mm(h_ref[1], x4_ref[128:320, :], NT)
    rh = mm(h_ref[0, 0:64], xh_ref[0:48, :], NT) + mm(h_ref[1, 0:64], xh_ref[32:80, :], NT)
    total = jnp.zeros((32, LANES), F32)
    for i in range(2):
        for j in range(2):
            part = r[(2 * i + j) * 32 : (2 * i + j + 1) * 32]
            for _ in range(2):
                piece = part.astype(BF)
                total = total + mm(piece, own_ref[i, j], NT)
                part = part - piece.astype(F32)
    for j in range(2):
        part = rh[j * 32 : (j + 1) * 32]
        for _ in range(2):
            piece = part.astype(BF)
            total = total + mm(piece, rim_ref[j], NT)
            part = part - piece.astype(F32)
    w_ref[320:352] = total
    first = core_ref[0] == 0

    @pl.when(first)
    def _():
        keep_ref[...] = w_ref[0:HALF].astype(BF)
        send_ref[...] = w_ref[HALF : 2 * HALF].astype(BF)

    @pl.when(jnp.logical_not(first))
    def _():
        keep_ref[...] = w_ref[HALF : 2 * HALF].astype(BF)
        send_ref[...] = w_ref[0:HALF].astype(BF)


def plane_kernel(in_ref, out_ref, d2_ref, d3_ref, loss_ref):
    total = in_ref[0, 0:HALF].astype(F32)
    for p in range(1, 16):
        total = total + in_ref[p, 0:HALF].astype(F32)
    out_ref[0:HALF] = total.astype(BF)

    def stack(k, yh):
        at = HALF + 16 * k
        return jnp.concatenate([in_ref[2 * p + yh, at : at + 16] for p in range(8)], axis=0)

    out1, gdense1, mixed = stack(0, 0), stack(1, 0), stack(2, 0)
    last = [stack(3, yh) for yh in range(2)]
    for yh in range(2):
        d1 = mm(last[yh], gdense1, TN)
        out_ref[HALF + 64 * yh : HALF + 64 * (yh + 1)] = d1[0:64].astype(BF)
    d2 = mm(out1, mixed, TN)
    d2_ref[...] = pltpu.roll(d2, 64, 1)[:, 0:64]
    d3 = mm(mixed, last[0], TN)
    d3_ref[...] = pltpu.roll(d3, 64, 1)[0:64, 0:4]
    lanes = lane_ids((128, LANES))
    rows = lax.broadcasted_iota(jnp.int32, (128, LANES), 0)
    held = jnp.logical_and(
        jnp.logical_and(lanes >= 68, lanes < 71), jnp.bitwise_and(rows, 15) == 0
    )
    values = jnp.where(held, last[0].astype(F32), 0.0)
    loss_ref[...] = jnp.sum(jnp.sum(values, axis=1, keepdims=True), axis=0, keepdims=True)


def depth_kernel(in_ref, out_ref):
    total = in_ref[0, 0:HALF].astype(F32)
    for p in range(1, 8):
        total = total + in_ref[p, 0:HALF].astype(F32)
    out_ref[0:HALF] = total.astype(BF)
    for p in range(8):
        out_ref[HALF + 128 * p : HALF + 128 * (p + 1)] = in_ref[p, HALF : HALF + 128]


def last_kernel(core_ref, mine_ref, other_ref, gw1_ref, gw2_ref, gd1_ref, w_ref):
    first = core_ref[0] == 0

    @pl.when(first)
    def _():
        w_ref[0:HALF] = mine_ref[0:HALF].astype(F32)
        w_ref[HALF : 2 * HALF] = other_ref[0:HALF].astype(F32)

    @pl.when(jnp.logical_not(first))
    def _():
        w_ref[0:HALF] = other_ref[0:HALF].astype(F32)
        w_ref[HALF : 2 * HALF] = mine_ref[0:HALF].astype(F32)

    for z in range(8):
        for yh in range(2):
            at = HALF + 128 * z + 64 * yh
            a = mine_ref[at : at + 64].astype(F32)
            b = other_ref[at : at + 64].astype(F32)
            slab = yh * 16 + z * 2
            gd1_ref[pl.ds(slab, 64, stride=32), :] = jnp.where(first, a, b)
            gd1_ref[pl.ds(slab + 1, 64, stride=32), :] = jnp.where(first, b, a)
    place = {1: 0, 2: 1, 0: 2}
    for a in range(3):
        for e in range(3):
            gw2_ref[a, 0, e] = jnp.zeros((64, 32), F32)
            for b in range(1, 3):
                if e < 2:
                    chunk, off = place[a], e * 64 + (b - 1) * 32
                else:
                    chunk = 4 if a == 0 else 3
                    off = (64 if a == 2 else 0) + (b - 1) * 32
                block = w_ref[chunk * 64 : (chunk + 1) * 64]
                if off:
                    block = pltpu.roll(block, LANES - off, 1)
                gw2_ref[a, b, e] = block[:, 0:32]
    block = w_ref[320:352]
    for a in range(3):
        for b in range(3):
            for e in range(3):
                off = ((a * 3 + b) * 3 + e) * 4
                moved = pltpu.roll(block, LANES - off, 1) if off else block
                gw1_ref[a, b, e] = moved[:, 0:4]


def call(kernel, outs, args, scratch=(), flops=0, scalars=0):
    vm = pl.BlockSpec(memory_space=pltpu.VMEM)
    sm = pl.BlockSpec(memory_space=pltpu.SMEM)
    size = sum(int(np.prod(s)) * jnp.dtype(d).itemsize for s, d in outs)
    return pl.pallas_call(
        kernel,
        out_shape=[jax.ShapeDtypeStruct(s, d) for s, d in outs],
        in_specs=[sm] * scalars + [vm] * (len(args) - scalars),
        out_specs=[vm] * len(outs),
        scratch_shapes=list(scratch),
        compiler_params=pltpu.CompilerParams(vmem_limit_bytes=40 * 1024 * 1024),
        cost_estimate=pl.CostEstimate(flops=flops, bytes_accessed=size, transcendentals=0),
    )(*args)


def local(volumes, targets, counts, w_conv1, w_conv2, w_dense1, w_dense2, w_dense3):
    core = lax.axis_index("core")
    position = lax.axis_index(SLABS)
    slabs = 32
    forward = [(i, i + 1) for i in range(slabs - 1)]
    backward = [(i + 1, i) for i in range(slabs - 1)]
    swap = [(0, 1), (1, 0)]

    rim = volumes[:, :, 3].reshape(256, 512)
    halo = lax.ppermute(rim, SLABS, forward)
    split = jnp.asarray(split_matrix(), BF)
    own_np, rim_np = band_matrices()
    own, rimsel = jnp.asarray(own_np, BF), jnp.asarray(rim_np, BF)
    w1 = jnp.pad(jnp.transpose(w_conv1, (3, 0, 1, 2, 4)).reshape(32, 108), ((0, 0), (0, 20)))
    w2 = jnp.transpose(w_conv2[:, 1:], (0, 3, 2, 1, 4)).reshape(3, 64, 192)

    x4, a1b, s1b, send = call(
        first_kernel,
        [((320, WIDE), BF), ((192, WIDE), BF), ((2, 64, WIDE), BF), ((64, WIDE), BF)],
        (volumes.reshape(1024, 512), split, w1, own, w2),
        flops=10**9,
    )
    part = lax.ppermute(send, SLABS, forward)
    xh, a1a, s1a, slope2, pay, fown = call(
        second_kernel,
        [
            ((80, WIDE), BF), ((192, WIDE), BF), ((2, 64, WIDE), BF), ((64, WIDE), BF),
            ((8, LANES), BF), ((S, LANES), BF),
        ],
        (halo, split, w1, own, rimsel, w2, x4, a1b, part),
        flops=10**9,
    )
    next2 = lax.ppermute(slope2, SLABS, backward)
    spread = jnp.broadcast_to(pay[None], (slabs, 8, LANES))
    gathered = lax.all_to_all(spread, SLABS, 0, 0, tiled=True)

    ends = jnp.cumsum(counts, dtype=jnp.int32)
    ids = jnp.arange(S, dtype=jnp.int32)
    owners = jnp.sum((ends[None, :] <= ids[:, None]).astype(jnp.int32), axis=1)
    alike = (owners[:, None] == owners[None, :]).astype(F32)
    same = alike / jnp.sum(alike, axis=1, keepdims=True)
    wd1 = jnp.transpose(w_dense1.reshape(64, slabs, 128), (1, 0, 2)).reshape(2048, 128)
    wd1own = lax.dynamic_slice(jnp.pad(wd1, ((0, 64), (0, 0))), (position * 64, 0), (128, 128))
    wd2 = jnp.pad(w_dense2, ((0, 0), (0, 64)))
    wd3 = jnp.pad(w_dense3, ((0, 64), (64, 60)))
    goal = jnp.pad(targets, ((0, 0), (64, 60)))
    tail, gf = call(
        tail_kernel,
        [((64, LANES), BF), ((128, S), F32)],
        (gathered, fown, wd1, wd1own, wd2, wd3, same, goal),
        flops=10**8,
    )

    w2t = jnp.transpose(w_conv2[:, 1:], (0, 2, 1, 4, 3)).reshape(3, 3, 64, 64)
    zero = jnp.zeros((64, 64), BF)
    block = jnp.concatenate(
        [
            jnp.concatenate(row, axis=1)
            for row in (
                (w2t[1, 1], zero, zero, zero),
                (w2t[2, 1], w2t[0, 1], zero, zero),
                (w2t[1, 2], zero, w2t[1, 0], zero),
                (w2t[2, 2], w2t[0, 2], w2t[2, 0], w2t[0, 0]),
            )
        ],
        axis=0,
    )
    which = core.astype(jnp.int32).reshape(1)
    keep, give = call(
        back_kernel,
        [((HALF, LANES), BF), ((HALF, LANES), BF)],
        (which, gf, slope2, next2, block, s1a, s1b, a1a, a1b, x4, xh, own, rimsel),
        scratch=[
            pltpu.VMEM((256, WIDE), BF), pltpu.VMEM((2, 128, WIDE), BF),
            pltpu.VMEM((2 * HALF, LANES), F32),
        ],
        flops=10**9,
        scalars=1,
    )
    taken = lax.ppermute(give, "core", swap)
    both = (keep.astype(F32) + taken.astype(F32)).astype(BF)
    rows = HALF + 64
    mixed = jnp.broadcast_to(jnp.concatenate([both, tail], axis=0)[None], (16, rows, LANES))
    planes = lax.all_to_all(mixed, PLANE, 0, 0, tiled=True)
    summed, d2, d3, loss = call(
        plane_kernel,
        [((HALF + 128, LANES), BF), ((128, 64), F32), ((64, 4), F32), ((1, 1), F32)],
        (planes,),
        flops=10**8,
    )
    deep = lax.all_to_all(
        jnp.broadcast_to(summed[None], (8, HALF + 128, LANES)), "z", 0, 0, tiled=True
    )
    (mine,) = call(depth_kernel, [((HALF + 1024, LANES), BF)], (deep,), flops=10**7)
    other = lax.ppermute(mine, "core", swap)
    gw1, gw2, gd1 = call(
        last_kernel,
        [((3, 3, 3, 32, 4), F32), ((3, 3, 3, 64, 32), F32), ((2048, 128), F32)],
        (which, mine, other),
        scratch=[pltpu.VMEM((2 * HALF, LANES), F32)],
        flops=10**7,
        scalars=1,
    )
    return loss.reshape(()), gw1, gw2, gd1, d2, d3


def solution(mesh):
    fine = Mesh(mesh.devices.reshape(4, 2, 2, 8, 2), ("x", "yl", "yh", "z", "core"))
    dp = ("x", "yl")
    placed = (P(dp, None, SLABS, None, None), P(dp, None), P(), P(), P(), P(), P(), P())
    return jax.shard_map(
        local, mesh=fine, in_specs=placed, out_specs=(P(), P(), P(), P(), P(), P()), check_vma=False
    )
```

```python
import functools

import jax
import jax.numpy as jnp
import numpy as np
from jax import lax
from jax.experimental import pallas as pl
from jax.experimental.pallas import tpu as pltpu
from jax.sharding import Mesh
from jax.sharding import PartitionSpec as P

BF = jnp.bfloat16
F32 = jnp.float32
SLABS = ("yh", "z", "core")
DP = ("x", "yl")
COLUMN = ("yh", "z")
S = 16
LANES = 128
WIDE = S * LANES
CHUNK = 512
PART = 24
HALF = 8 * PART
BIG = 60 * 1024 * 1024
SMALL = 16 * 1024 * 1024

NN = (((1,), (0,)), ((), ()))
NT = (((1,), (1,)), ((), ()))
TN = (((0,), (0,)), ((), ()))


def mm(a, b, dims=NN):
    return lax.dot_general(a, b, dims, preferred_element_type=F32)


def mm_exact(a, b):
    return lax.dot_general(
        a, b, NN, preferred_element_type=F32, precision=lax.Precision.HIGHEST
    )


def leaky(v, t):
    return v * (0.65 + 0.35 * t)


def slope(v, t):
    return 0.65 + 0.35 * t + 0.35 * v * (1.0 - t * t)


@functools.cache
def split_matrix():
    m = np.zeros((512, 640), np.float32)
    for k, offset in enumerate((-1, 0, 1, 2, 3)):
        for i in range(128):
            if 4 * i + offset >= 0:
                m[4 * i + offset, k * 128 + i] = 1.0
    return m


@functools.cache
def band_matrices():
    own = np.zeros((2, 2, 108, 192), np.float32)
    rim = np.zeros((2, 108, 48), np.float32)
    own_back = np.zeros((2, 2, 128, 192), np.float32)
    rim_back = np.zeros((2, 128, 48), np.float32)
    for i in range(2):
        for j in range(2):
            for a in range(3):
                for b in range(3):
                    x, y = 2 * i + a - 1, 2 * j + b - 1
                    if y < 0:
                        continue
                    for e in range(3):
                        for c in range(4):
                            tap = (a * 3 + b) * 3 + e
                            if x >= 0:
                                col = ((e * 4 + c) * 4 + x) * 4 + y
                                own[i, j, tap * 4 + c, col] = 1.0
                                own_back[i, j, c * 32 + tap, col] = 1.0
                            else:
                                col = (e * 4 + c) * 4 + y
                                rim[j, tap * 4 + c, col] = 1.0
                                rim_back[j, c * 32 + tap, col] = 1.0
    return own, rim, own_back, rim_back


def lane_ids(shape):
    return lax.broadcasted_iota(jnp.int32, shape, len(shape) - 1)


def shift_up(x):
    parts = []
    for k in range(x.shape[1] // LANES):
        p = pltpu.roll(x[:, k * LANES : (k + 1) * LANES], 1, 1)
        parts.append(jnp.where(lane_ids(p.shape) == 0, 0.0, p))
    return jnp.concatenate(parts, axis=1)


def shift_down(x):
    parts = []
    for k in range(x.shape[1] // LANES):
        p = pltpu.roll(x[:, k * LANES : (k + 1) * LANES], LANES - 1, 1)
        parts.append(jnp.where(lane_ids(p.shape) == LANES - 1, 0.0, p))
    return jnp.concatenate(parts, axis=1)


class Feed:
    def __init__(self, sources, buffers, sems):
        self.copies = [
            pltpu.make_async_copy(s, b, sems.at[k])
            for k, (s, b) in enumerate(zip(sources, buffers, strict=True))
        ]
        self.buffers, self.done = buffers, set()
        for copy in self.copies:
            copy.start()

    def __getitem__(self, k):
        if k not in self.done:
            self.copies[k].wait()
            self.done.add(k)
        return self.buffers[k]


def call(kernel, outs, args, scalars=(), scratch=(), vmem=BIG, flops=10**8):
    args = [a if isinstance(a, tuple) else (a, 1) for a in args]
    n_in, n_sc, n_out = len(args), len(scalars), len(outs)
    pieces = [(k, p, a.shape[0] // n) for k, (a, n) in enumerate(args) for p in range(n)]
    early = [k for k, o in enumerate(outs) if o[2]]

    def body(*refs):
        scalar_refs, refs = refs[:n_sc], refs[n_sc:]
        ins, refs = refs[:n_in], refs[n_in:]
        out_refs, refs = refs[:n_out], refs[n_out:]
        buffers, refs = refs[:n_in], refs[n_in:]
        held, refs = refs[: len(early)], refs[len(early) :]
        in_sems, out_sems, extra = refs[0], refs[1], refs[2:]

        def cut(ref, k, p, size):
            return ref if args[k][1] == 1 else ref.at[pl.ds(p * size, size)]

        feed = Feed(
            [cut(ins[k], k, p, s) for k, p, s in pieces],
            [cut(buffers[k], k, p, s) for k, p, s in pieces],
            in_sems,
        )
        local_outs = list(out_refs)
        for n, k in enumerate(early):
            local_outs[k] = held[n]
        sent = []

        def send(k):
            n = early.index(k)
            copy = pltpu.make_async_copy(held[n], out_refs[k], out_sems.at[n])
            copy.start()
            sent.append(copy)

        kernel(scalar_refs, feed, local_outs, send, *extra)
        for copy in sent:
            copy.wait()

    size = sum(int(np.prod(o[0])) * jnp.dtype(o[1]).itemsize for o in outs)
    return pl.pallas_call(
        body,
        out_shape=[jax.ShapeDtypeStruct(o[0], o[1]) for o in outs],
        in_specs=[pl.BlockSpec(memory_space=pltpu.SMEM)] * n_sc
        + [pl.BlockSpec(memory_space=pl.ANY)] * n_in,
        out_specs=[
            pl.BlockSpec(memory_space=pl.ANY if o[2] else pltpu.VMEM) for o in outs
        ],
        scratch_shapes=[pltpu.VMEM(a.shape, a.dtype) for a, _ in args]
        + [pltpu.VMEM(outs[k][0], outs[k][1]) for k in early]
        + [pltpu.SemaphoreType.DMA((len(pieces),)), pltpu.SemaphoreType.DMA((max(len(early), 1),))]
        + list(scratch),
        compiler_params=pltpu.CompilerParams(vmem_limit_bytes=vmem),
        cost_estimate=pl.CostEstimate(flops=flops, bytes_accessed=size, transcendentals=0),
    )(*scalars, *[a for a, _ in args])


def store_plane(h, s, cols, a1_ref, slope_ref):
    t = jnp.tanh(h)
    act = leaky(h, t)
    slope_ref[s, :, cols] = slope(h, t).astype(BF)
    if s == 0:
        a1_ref[64:128, cols] = act.astype(BF)
    else:
        a1_ref[128:192, cols] = act.astype(BF)
        a1_ref[0:64, cols] = shift_up(act).astype(BF)


def taps_of(w2_ref, a):
    return jnp.concatenate([w2_ref[a, b, e] for e in range(3) for b in (1, 2)], axis=0)


def first_kernel(scalars, feed, outs, send):
    x4_ref, a1_ref, slope_ref, send_ref = outs
    split, w1, own = feed[4], feed[5], feed[6]
    taps = w1[...].reshape(108, 32)
    w = jnp.concatenate([mm(taps, own[1, j], TN).astype(BF) for j in range(2)], axis=0)
    for q in range(4):
        v = feed[q]
        rows = jnp.concatenate([v[n].reshape(64, 512) for n in range(4)], axis=0)
        d = mm(rows, split[...])
        for k in range(5):
            for n in range(4):
                x4_ref[k * 64 : (k + 1) * 64, (4 * q + n) * LANES : (4 * q + n + 1) * LANES] = d[
                    n * 64 : (n + 1) * 64, k * LANES : (k + 1) * LANES
                ].astype(BF)
    send(0)
    w2 = taps_of(feed[7], 0)
    for q in range(4):
        cols = slice(q * CHUNK, (q + 1) * CHUNK)
        for s in range(2):
            h = mm(w, x4_ref[s * 128 : s * 128 + 192, cols])
            store_plane(h, s, cols, a1_ref, slope_ref)
        send_ref[:, cols] = mm(w2, a1_ref[:, cols], TN).astype(BF)
    send(1)
    send(2)


def second_kernel(scalars, feed, outs, send, wide_ref):
    xh_ref, a1_ref, slope_ref, part_ref, wd1_ref, block_ref = outs
    halo, split, w1, own, rim, w2 = (feed[k] for k in range(6))
    taps = w1[...].reshape(108, 32)
    w = jnp.concatenate([mm(taps, own[0, j], TN).astype(BF) for j in range(2)], axis=0)
    wh = jnp.concatenate([mm(taps, rim[j], TN).astype(BF) for j in range(2)], axis=0)
    rows = jnp.concatenate([halo[n].reshape(16, 512) for n in range(S)], axis=0)
    d = mm(rows, split[...])
    for k in range(5):
        for n in range(S):
            xh_ref[k * 16 : (k + 1) * 16, n * LANES : (n + 1) * LANES] = d[
                n * 16 : (n + 1) * 16, k * LANES : (k + 1) * LANES
            ].astype(BF)
    send(0)
    w2a, w2b = taps_of(w2, 1), taps_of(w2, 2)
    x4, a1b = feed[6], feed[7]
    for q in range(4):
        cols = slice(q * CHUNK, (q + 1) * CHUNK)
        for s in range(2):
            h = mm(w, x4[s * 128 : s * 128 + 192, cols]) + mm(
                wh, xh_ref[s * 32 : s * 32 + 48, cols]
            )
            store_plane(h, s, cols, a1_ref, slope_ref)
        part_ref[:, cols] = mm(w2a, a1_ref[:, cols], TN) + mm(w2b, a1b[:, cols], TN)
    for k in (1, 2, 3):
        send(k)
    wide_ref[...] = feed[8][...].astype(F32)
    for x in range(32):
        wd1_ref[x * 64 : (x + 1) * 64] = wide_ref[pl.ds(x, 64, stride=32), :].astype(BF)
    wd1_ref[2048:2112] = jnp.zeros((64, LANES), BF)
    send(4)

    def tap(a, e):
        return jnp.concatenate([w2[a, 1, e], w2[a, 2, e]], axis=0)

    zero = jnp.zeros((64, 64), BF)
    for k, row in enumerate(
        (
            (tap(1, 1), zero, zero, zero),
            (tap(2, 1), tap(0, 1), zero, zero),
            (tap(1, 2), zero, tap(1, 0), zero),
            (tap(2, 2), tap(0, 2), tap(2, 0), tap(0, 0)),
        )
    ):
        block_ref[k * 64 : (k + 1) * 64] = jnp.concatenate(row, axis=1)
    send(5)


def third_kernel(scalars, feed, outs, send):
    slope2_ref, pay_ref, fown_ref = outs
    part, got = feed[0], feed[1]
    total = jnp.zeros((S, 64), F32)
    for q in range(4):
        cols = slice(q * CHUNK, (q + 1) * CHUNK)
        h2 = part[:, cols] + got[:, cols].astype(F32)
        t = jnp.tanh(h2)
        act2 = leaky(h2, t).astype(BF)
        slope2_ref[:, cols] = slope(h2, t).astype(BF)
        rows = lax.broadcasted_iota(jnp.int32, (S, CHUNK), 0)
        owner = lax.shift_right_logical(lane_ids((S, CHUNK)), 7) + 4 * q
        pick = jnp.where(rows == owner, 1.0, 0.0).astype(BF)
        total = total + mm(pick, act2, NT)
    feats = total * (1.0 / 128.0)
    pay = jnp.concatenate([feats[0:8], feats[8:16]], axis=1).astype(BF)
    for x in range(32):
        pay_ref[x] = pay
    fown_ref[...] = jnp.concatenate([feats, jnp.zeros((S, 64), F32)], axis=1).astype(BF)


def tail(scalars, feed, padded_ref):
    counts, position = scalars[0], scalars[1]
    ends = []
    for k in range(32):
        ends.append(counts[k] + (ends[-1] if k else 0))
    by_row = lax.broadcasted_iota(jnp.int32, (S, S), 0)
    by_col = lax.broadcasted_iota(jnp.int32, (S, S), 1)
    row_owner = jnp.zeros((S, S), jnp.int32)
    col_owner = jnp.zeros((S, S), jnp.int32)
    for end in ends:
        row_owner = row_owner + jnp.where(by_row >= end, 1, 0)
        col_owner = col_owner + jnp.where(by_col >= end, 1, 0)
    alike = jnp.where(row_owner == col_owner, 1.0, 0.0)
    same = alike / jnp.sum(alike, axis=1, keepdims=True)

    w2 = jnp.concatenate([feed[3][...], jnp.zeros((64, LANES), BF)], axis=0)
    padded_ref[...] = jnp.zeros((LANES, LANES), F32)
    padded_ref[64:68, 0:64] = feed[4][...].astype(F32)
    w3 = padded_ref[...].astype(BF)
    padded_ref[...] = jnp.zeros((LANES, LANES), F32)
    padded_ref[64:68, 0:S] = feed[5][...]
    goal = jnp.transpose(padded_ref[...], (1, 0))[0:S]

    low = lane_ids((8, LANES)) < 64
    g, pairs = feed[0], []
    for p in range(16):
        ga, gb = g[2 * p].astype(F32), g[2 * p + 1].astype(F32)
        lo = jnp.where(low, ga, pltpu.roll(gb, 64, 1))
        hi = jnp.where(low, pltpu.roll(ga, 64, 1), gb)
        pairs.append(jnp.concatenate([lo, hi], axis=0).astype(BF))
    feats = jnp.concatenate(pairs, axis=1)
    wd1 = feed[2]
    dense1 = mm(feats, wd1[0:2048])
    centred = dense1 - 0.5 * mm_exact(same, dense1)
    t1 = jnp.tanh(centred)
    out1 = leaky(centred, t1).astype(BF)
    dense2 = mm(out1, w2, NT)
    t2 = jnp.tanh(dense2)
    out2 = leaky(dense2, t2).astype(BF)
    diff = mm(out2, w3, NT) - goal
    loss = jnp.sum(jnp.sum(diff * diff, axis=1, keepdims=True), axis=0, keepdims=True) / 32.0
    gpred = (diff / 16.0).astype(BF)
    gdense2 = (mm(gpred, w3) * slope(dense2, t2)).astype(BF)
    gcentred = mm(gdense2, w2) * slope(centred, t1)
    gdense1 = (gcentred - 0.5 * mm_exact(same, gcentred)).astype(BF)
    at = pl.multiple_of(position[0] * 64, 64)
    gfeats = mm(wd1[pl.ds(at, LANES), :], gdense1, NT)
    return out1, out2, gpred, gdense2, gdense1, gfeats, loss


def split_loss(loss):
    high = loss.astype(BF).astype(F32)
    mid = (loss - high).astype(BF).astype(F32)
    return high, mid, loss - high - mid


def back_kernel(scalars, feed, outs, send, padded_ref, g_ref, h_ref, w_ref):
    keep_ref, give_ref, own_ref = outs
    core = scalars[2]
    out1, out2, gpred, gdense2, gdense1, gfeats, loss = tail(scalars, feed, padded_ref)
    gf = gfeats.astype(BF).astype(F32) * (1.0 / 128.0)
    slope2, next2, block = feed[6], feed[7], feed[8]
    s1 = (feed[9], feed[10])
    for q in range(4):
        cols = slice(q * CHUNK, (q + 1) * CHUNK)
        spread = jnp.concatenate(
            [
                jnp.broadcast_to(gf[:, 4 * q + n : 4 * q + n + 1], (128, LANES))
                for n in range(4)
            ],
            axis=1,
        )
        go = spread[0:64] * slope2[:, cols].astype(F32)
        gn = spread[64:128] * next2[:, cols].astype(F32)
        g_ref[0:64, cols] = go.astype(BF)
        g_ref[64:128, cols] = gn.astype(BF)
        g_ref[128:192, cols] = shift_down(go).astype(BF)
        g_ref[192:256, cols] = shift_down(gn).astype(BF)
        gact = mm(block[...], g_ref[:, cols])
        for s in range(2):
            for i in range(2):
                r = (2 * s + i) * 64
                h_ref[s, i * 64 : (i + 1) * 64, cols] = (
                    gact[r : r + 64] * s1[i][s, :, cols].astype(F32)
                ).astype(BF)
    a1a, a1b = feed[11], feed[12]
    w_ref[0:192] = mm(a1b[...], g_ref[0:128, :], NT)
    a1 = mm(a1a[...], g_ref[0:64, :], NT)
    w_ref[192:288] = jnp.concatenate([a1[0:96], a1[96:192]], axis=1)
    x4, xh = feed[13], feed[14]
    r = mm(x4[0:192, :], h_ref[0], NT) + mm(x4[128:320, :], h_ref[1], NT)
    rh = mm(xh[0:48, :], h_ref[0], NT) + mm(xh[32:80, :], h_ref[1], NT)
    own, rim = feed[15], feed[16]
    r_high, rh_high = r.astype(BF), rh.astype(BF)
    r_low, rh_low = (r - r_high.astype(F32)).astype(BF), (rh - rh_high.astype(F32)).astype(BF)
    group = lax.shift_right_logical(lane_ids((LANES, LANES)), 5)
    taps = jnp.zeros((LANES, LANES), F32)
    for i in range(2):
        for j in range(2):
            part = mm(own[i, j], r_high) + mm(own[i, j], r_low)
            if i == 0:
                part = part + mm(rim[j], rh_high) + mm(rim[j], rh_low)
            taps = jnp.where(group == 2 * i + j, part, taps)
    taps = taps + pltpu.roll(taps, 64, 1)
    taps = taps + pltpu.roll(taps, 32, 1)
    packed = taps[0:32]
    for c in range(1, 4):
        packed = jnp.where(group[0:32] == c, taps[c * 32 : (c + 1) * 32], packed)
    w_ref[288:320] = packed
    w_ref[320:384] = jnp.zeros((64, LANES), F32)
    first = core[0] == 0

    @pl.when(first)
    def _():
        keep_ref[...] = w_ref[0:HALF].astype(BF)
        give_ref[...] = w_ref[HALF : 2 * HALF].astype(BF)

    @pl.when(jnp.logical_not(first))
    def _():
        keep_ref[...] = w_ref[HALF : 2 * HALF].astype(BF)
        give_ref[...] = w_ref[0:HALF].astype(BF)

    own_ref[0:64] = mm(feed[1][...], gdense1, TN)[0:64].astype(BF)
    own_ref[64:128] = mm(gdense2, out1, TN)[0:64].astype(BF)
    d3 = mm(gpred, out2, TN)[64:72]
    lanes = lane_ids((8, LANES))
    top = lax.broadcasted_iota(jnp.int32, (8, LANES), 0) == 0
    for k, piece in enumerate(split_loss(loss)):
        d3 = jnp.where(jnp.logical_and(top, lanes == 64 + k), piece, d3)
    own_ref[128:136] = d3.astype(BF)
    own_ref[136:144] = jnp.zeros((8, LANES), BF)


def spread_kernel(scalars, feed, outs, send):
    (out_ref,) = outs
    keep, own, taken = feed[0], feed[1], feed[2]
    both = keep[...].astype(F32) + taken[...].astype(F32)
    mine = own[...].astype(F32)
    for k in range(8):
        out_ref[k] = jnp.concatenate(
            [
                both[k * PART : (k + 1) * PART],
                mine[128:136],
                mine[k * 8 : (k + 1) * 8],
                mine[64 + k * 8 : 72 + k * 8],
            ],
            axis=0,
        ).astype(BF)


def group_kernel(scalars, feed, outs, send):
    out_ref, d2_ref, d3_ref, loss_ref = outs
    got = feed[0]
    total = got[0].astype(F32)
    for k in range(1, 8):
        total = total + got[k].astype(F32)
    pay = jnp.concatenate([total[0:PART], total[32:40]], axis=0).astype(BF)
    for k in range(16):
        out_ref[k] = pay
    d2_ref[...] = total[40:48]
    small = total[PART:32]
    d3_ref[...] = small[0:4, 0:64]
    lanes = lane_ids((8, LANES))
    rows = lax.broadcasted_iota(jnp.int32, (8, LANES), 0)
    held = jnp.logical_and(jnp.logical_and(lanes >= 64, lanes < 67), rows == 0)
    values = jnp.where(held, small, 0.0)
    loss_ref[...] = jnp.sum(jnp.sum(values, axis=1, keepdims=True), axis=0, keepdims=True)


def column_kernel(scalars, feed, outs, send):
    (out_ref,) = outs
    got, d2 = feed[0], feed[1]
    blocks = [got[k].astype(F32) for k in range(16)]
    total = blocks[0][0:PART]
    for b in blocks[1:]:
        total = total + b[0:PART]
    pay = jnp.concatenate([total, d2[...]] + [b[PART:32] for b in blocks], axis=0).astype(BF)
    for k in range(8):
        out_ref[k] = pay


def last_kernel(scalars, feed, outs, send, w_ref, t_ref):
    gw1_ref, gw2_ref, gd1_ref, gd2_ref = outs
    mine, other = feed[0], feed[1]
    first = scalars[0][0] == 0
    for k in range(8):
        a, b = mine[k].astype(F32), other[k].astype(F32)
        low, high = jnp.where(first, a, b), jnp.where(first, b, a)
        w_ref[k * PART : (k + 1) * PART] = low[0:PART]
        w_ref[HALF + k * PART : HALF + (k + 1) * PART] = high[0:PART]
        gd2_ref[k * 8 : (k + 1) * 8] = a[PART:32]
        for slab in range(16):
            at = 32 + 8 * slab
            row = k * 256 + 2 * slab
            gd1_ref[pl.ds(row, 8, stride=32), :] = low[at : at + 8]
            gd1_ref[pl.ds(row + 1, 8, stride=32), :] = high[at : at + 8]
    send(2)
    for a in range(3):
        for e in range(3):
            gw2_ref[a, 0, e] = jnp.zeros((32, 64), F32)
            for b in (1, 2):
                at = e * 64 + (b - 1) * 32
                right = a == 0
                if a == 1:
                    right = at >= 96
                    at = 192 + at % 96
                block = w_ref[at : at + 32]
                if right:
                    block = pltpu.roll(block, 64, 1)
                gw2_ref[a, b, e] = block[:, 0:64]
    packed = w_ref[288:320]
    for c in range(4):
        t_ref[c * 32 : (c + 1) * 32] = pltpu.roll(packed, (LANES - 32 * c) % LANES, 1)
    for a in range(3):
        for b in range(3):
            for e in range(3):
                tap = (a * 3 + b) * 3 + e
                gw1_ref[a, b, e] = t_ref[pl.ds(tap, 4, stride=32), :][:, 0:32]


def local(volumes, targets, counts, w_conv1, w_conv2, w_dense1, w_dense2, w_dense3):
    core = lax.axis_index("core").astype(jnp.int32).reshape(1)
    position = lax.axis_index(SLABS).astype(jnp.int32).reshape(1)
    forward = [(i, i + 1) for i in range(31)]
    backward = [(i + 1, i) for i in range(31)]
    swap = [(0, 1), (1, 0)]
    split = jnp.asarray(split_matrix(), BF)
    own, rim, own_back, rim_back = (jnp.asarray(m, BF) for m in band_matrices())
    w1 = jnp.swapaxes(w_conv1, 3, 4).reshape(27, 4, 32)
    w2 = jnp.swapaxes(w_conv2, 3, 4)

    halo = lax.ppermute(volumes[:, :, 3], SLABS, forward)
    x4, a1b, s1b, away = call(
        first_kernel,
        [
            ((320, WIDE), BF, True), ((192, WIDE), BF, True), ((2, 64, WIDE), BF, True),
            ((64, WIDE), BF, False),
        ],
        ((volumes, 4), split, w1, own, w2),
        flops=10**9,
    )
    got = lax.ppermute(away, SLABS, forward)
    xh, a1a, s1a, part, wd1, block = call(
        second_kernel,
        [
            ((80, WIDE), BF, True), ((192, WIDE), BF, True), ((2, 64, WIDE), BF, True),
            ((64, WIDE), F32, True), ((2112, LANES), BF, True), ((256, 256), BF, True),
        ],
        (halo, split, w1, own, rim, w2, x4, a1b, w_dense1),
        scratch=[pltpu.VMEM((2048, LANES), F32)],
        flops=2 * 10**9,
    )
    slope2, pay, fown = call(
        third_kernel,
        [((64, WIDE), BF, False), ((32, 8, LANES), BF, False), ((S, LANES), BF, False)],
        (part, got),
    )
    gathered = lax.all_to_all(pay, SLABS, 0, 0, tiled=True)
    next2 = lax.ppermute(slope2, SLABS, backward)
    keep, give, mine = call(
        back_kernel,
        [((HALF, LANES), BF, False), ((HALF, LANES), BF, False), ((144, LANES), BF, False)],
        (
            gathered, fown, wd1, w_dense2.T, w_dense3.T, targets.T, slope2, next2, block,
            s1a, s1b, a1a, a1b, x4, xh, own_back, rim_back,
        ),
        scalars=(counts, position, core),
        scratch=[
            pltpu.VMEM((LANES, LANES), F32), pltpu.VMEM((256, WIDE), BF),
            pltpu.VMEM((2, 128, WIDE), BF), pltpu.VMEM((2 * HALF, LANES), F32),
        ],
        flops=2 * 10**9,
    )
    taken = lax.ppermute(give, "core", swap)
    (scattered,) = call(
        spread_kernel, [((8, 48, LANES), BF, False)], (keep, mine, taken), vmem=SMALL
    )
    over_dp = lax.all_to_all(scattered, DP, 0, 0, tiled=True)
    to_column, d2, d3, loss = call(
        group_kernel,
        [((16, 32, LANES), BF, False), ((8, LANES), F32, False), ((4, 64), F32, False), ((1, 1), F32, False)],
        (over_dp,),
        vmem=SMALL,
    )
    over_column = lax.all_to_all(to_column, COLUMN, 0, 0, tiled=True)
    (back,) = call(
        column_kernel, [((8, 160, LANES), BF, False)], (over_column, d2), vmem=SMALL
    )
    summed = lax.all_to_all(back, DP, 0, 0, tiled=True)
    other = lax.ppermute(summed, "core", swap)
    gw1, gw2, gd1, gd2 = call(
        last_kernel,
        [
            ((3, 3, 3, 4, 32), F32, False), ((3, 3, 3, 32, 64), F32, False),
            ((2048, LANES), F32, True), ((64, LANES), F32, False),
        ],
        (summed, other),
        scalars=(core,),
        scratch=[pltpu.VMEM((2 * HALF, LANES), F32), pltpu.VMEM((LANES, LANES), F32)],
        vmem=SMALL,
    )
    return (
        loss.reshape(()), jnp.swapaxes(gw1, 3, 4), jnp.swapaxes(gw2, 3, 4), gd1, gd2.T, d3.T,
    )


def solution(mesh):
    fine = Mesh(mesh.devices.reshape(4, 2, 2, 8, 2), ("x", "yl", "yh", "z", "core"))
    placed = (P(DP, None, SLABS, None, None), P(DP, None), P(), P(), P(), P(), P(), P())
    return jax.shard_map(
        local, mesh=fine, in_specs=placed, out_specs=(P(), P(), P(), P(), P(), P()), check_vma=False
    )
```

```python
import functools

import jax
import jax.numpy as jnp
import numpy as np
from jax import lax
from jax.experimental import pallas as pl
from jax.experimental.pallas import tpu as pltpu
from jax.sharding import Mesh
from jax.sharding import PartitionSpec as P

BF = jnp.bfloat16
F32 = jnp.float32
SLABS = ("yh", "z", "core")
DP = ("x", "yl")
COLUMN = ("yh", "z")
S = 16
LANES = 128
WIDE = S * LANES
CHUNK = 512
PART = 24
SMALL = 16 * 1024 * 1024

NN = (((1,), (0,)), ((), ()))
NT = (((1,), (1,)), ((), ()))
TN = (((0,), (0,)), ((), ()))


def mm(a, b, dims=NN):
    return lax.dot_general(a, b, dims, preferred_element_type=F32)


def mm_exact(a, b):
    return lax.dot_general(
        a, b, NN, preferred_element_type=F32, precision=lax.Precision.HIGHEST
    )


def leaky(v, t):
    return v * (0.65 + 0.35 * t)


def slope(v, t):
    return 0.65 + 0.35 * t + 0.35 * v * (1.0 - t * t)


@functools.cache
def split_matrix():
    m = np.zeros((512, 640), np.float32)
    for k, offset in enumerate((-1, 0, 1, 2, 3)):
        for i in range(128):
            if 4 * i + offset >= 0:
                m[4 * i + offset, k * 128 + i] = 1.0
    return m


@functools.cache
def band_matrices():
    own = np.zeros((2, 2, 108, 192), np.float32)
    rim = np.zeros((2, 108, 48), np.float32)
    for i in range(2):
        for j in range(2):
            for a in range(3):
                for b in range(3):
                    x, y = 2 * i + a - 1, 2 * j + b - 1
                    if y < 0:
                        continue
                    for e in range(3):
                        for c in range(4):
                            src = ((a * 3 + b) * 3 + e) * 4 + c
                            if x >= 0:
                                own[i, j, src, ((e * 4 + c) * 4 + x) * 4 + y] = 1.0
                            else:
                                rim[j, src, (e * 4 + c) * 4 + y] = 1.0
    return own, rim


def lane_ids(shape):
    return lax.broadcasted_iota(jnp.int32, shape, len(shape) - 1)


def shift_up(x):
    parts = []
    for k in range(x.shape[1] // LANES):
        p = pltpu.roll(x[:, k * LANES : (k + 1) * LANES], 1, 1)
        parts.append(jnp.where(lane_ids(p.shape) == 0, 0.0, p))
    return jnp.concatenate(parts, axis=1)


def shift_down(x):
    parts = []
    for k in range(x.shape[1] // LANES):
        p = pltpu.roll(x[:, k * LANES : (k + 1) * LANES], LANES - 1, 1)
        parts.append(jnp.where(lane_ids(p.shape) == LANES - 1, 0.0, p))
    return jnp.concatenate(parts, axis=1)


def call(kernel, outs, args, scalars=(), scratch=(), vmem=SMALL, flops=10**8):
    size = sum(int(np.prod(s)) * jnp.dtype(d).itemsize for s, d in outs)
    return pl.pallas_call(
        kernel,
        out_shape=[jax.ShapeDtypeStruct(s, d) for s, d in outs],
        in_specs=[pl.BlockSpec(memory_space=pltpu.SMEM)] * len(scalars)
        + [pl.BlockSpec(memory_space=pltpu.VMEM)] * len(args),
        out_specs=[pl.BlockSpec(memory_space=pltpu.VMEM)] * len(outs),
        scratch_shapes=list(scratch),
        compiler_params=pltpu.CompilerParams(vmem_limit_bytes=vmem),
        cost_estimate=pl.CostEstimate(flops=flops, bytes_accessed=size, transcendentals=0),
    )(*scalars, *args)


def parts(ref, *heights):
    out, at = [], 0
    for h in heights:
        out.append(ref.at[at : at + h])
        at += h
    return out


def bands(taps, ref, *index):
    return jnp.concatenate([mm(taps, ref[(*index, j)], TN).astype(BF) for j in range(2)], axis=0)


def split_here():
    z = lax.broadcasted_iota(jnp.int32, (512, LANES), 0)
    m = lax.broadcasted_iota(jnp.int32, (512, LANES), 1)
    return jnp.concatenate(
        [jnp.where(z - 4 * m == k - 1, 1.0, 0.0).astype(BF) for k in range(5)], axis=1
    )


def band_here(i, j):
    row = lax.broadcasted_iota(jnp.int32, (108, 1), 0)
    tap = lax.shift_right_logical(row, 2)
    third = lax.shift_right_logical(tap * 43, 7)
    a = lax.shift_right_logical(third * 43, 7)
    e, b = tap - 3 * third, third - 3 * a
    row_key = (e * 4 + jnp.bitwise_and(row, 3)) * 64 + a * 8 + b
    col = lax.broadcasted_iota(jnp.int32, (1, 192), 1)
    x = jnp.bitwise_and(lax.shift_right_logical(col, 2), 3) - 2 * i + 1
    y = jnp.bitwise_and(col, 3) - 2 * j + 1
    col_key = lax.shift_right_logical(col, 4) * 64 + x * 8 + y
    return jnp.where(row_key == col_key, 1.0, 0.0).astype(BF)


def store_plane(h, s, cols, a1_ref, slope_ref):
    t = jnp.tanh(h)
    act = leaky(h, t)
    slope_ref[s * 64 : (s + 1) * 64, cols] = slope(h, t).astype(BF)
    if s == 0:
        a1_ref[64:128, cols] = act.astype(BF)
    else:
        a1_ref[128:192, cols] = act.astype(BF)
        a1_ref[0:64, cols] = shift_up(act).astype(BF)


def taps_of(w2_ref, a):
    return jnp.concatenate([w2_ref[a, b, e] for e in range(3) for b in (1, 2)], axis=0)


def bands(taps, ref, *index):
    return jnp.concatenate([mm(taps, ref[(*index, j)], TN).astype(BF) for j in range(2)], axis=0)


OWN = (320, 192)
NEAR = (80, 192, 128)


def separate(rows, split, out_ref, height, first, many):
    d = mm(rows, split[...])
    for k in range(5):
        for n in range(many):
            at = (first + n) * LANES
            out_ref[k * height : (k + 1) * height, at : at + LANES] = d[
                n * height : (n + 1) * height, k * LANES : (k + 1) * LANES
            ].astype(BF)


def first_kernel(v, w1, w2, out_ref, slope_ref, away_ref):
    x4_ref, a1_ref = parts(out_ref, *OWN)
    split = split_here()
    w = bands(w1[...].reshape(108, 32), {(j,): band_here(1, j) for j in range(2)})
    w2a = taps_of(w2, 0)
    for q in range(4):
        rows = jnp.concatenate([v[4 * q + n].reshape(64, 512) for n in range(4)], axis=0)
        separate(rows, split, x4_ref, 64, 4 * q, 4)
        cols = slice(q * CHUNK, (q + 1) * CHUNK)
        for s in range(2):
            h = mm(w, x4_ref[s * 128 : s * 128 + 192, cols])
            store_plane(h, s, cols, a1_ref, slope_ref)
        away_ref[:, cols] = mm(w2a, a1_ref[:, cols], TN).astype(BF)


def second_kernel(
    halo, split, w1, own, rim, w2, first_ref, wd1, out_ref, part_ref, wd1_ref, block_ref, wide_ref
):
    x4, a1c = parts(first_ref, *OWN)
    xh_ref, a1_ref, slope_ref = parts(out_ref, *NEAR)
    taps = w1[...].reshape(108, 32)
    w, wh = bands(taps, own, 0), bands(taps, rim)
    rows = jnp.concatenate([halo[n].reshape(16, 512) for n in range(S)], axis=0)
    separate(rows, split, xh_ref, 16, 0, S)
    taps_b, taps_c = taps_of(w2, 1), taps_of(w2, 2)
    for q in range(4):
        cols = slice(q * CHUNK, (q + 1) * CHUNK)
        for s in range(2):
            h = mm(w, x4[s * 128 : s * 128 + 192, cols]) + mm(
                wh, xh_ref[s * 32 : s * 32 + 48, cols]
            )
            store_plane(h, s, cols, a1_ref, slope_ref)
        part_ref[:, cols] = mm(taps_b, a1_ref[:, cols], TN) + mm(taps_c, a1c[:, cols], TN)

    def tap(a, e):
        return jnp.concatenate([w2[a, 1, e], w2[a, 2, e]], axis=0)

    zero = jnp.zeros((64, 64), BF)
    for k, row in enumerate(
        (
            (tap(1, 1), zero, zero, zero),
            (tap(2, 1), tap(0, 1), zero, zero),
            (tap(1, 2), zero, tap(1, 0), zero),
            (tap(2, 2), tap(0, 2), tap(2, 0), tap(0, 0)),
        )
    ):
        block_ref[k * 64 : (k + 1) * 64] = jnp.concatenate(row, axis=1)
    wide_ref[...] = wd1[...].astype(F32)
    for x in range(32):
        wd1_ref[x * 64 : (x + 1) * 64] = wide_ref[pl.ds(x, 64, stride=32), :].astype(BF)


def third_kernel(part, got, slope2_ref, pay_ref, fown_ref):
    total = jnp.zeros((S, 64), F32)
    for q in range(4):
        cols = slice(q * CHUNK, (q + 1) * CHUNK)
        h2 = part[:, cols] + got[:, cols].astype(F32)
        t = jnp.tanh(h2)
        act2 = leaky(h2, t).astype(BF)
        slope2_ref[:, cols] = slope(h2, t).astype(BF)
        rows = lax.broadcasted_iota(jnp.int32, (S, CHUNK), 0)
        owner = lax.shift_right_logical(lane_ids((S, CHUNK)), 7) + 4 * q
        pick = jnp.where(rows == owner, 1.0, 0.0).astype(BF)
        total = total + mm(pick, act2, NT)
    feats = total * (1.0 / 128.0)
    pay = jnp.concatenate([feats[0:8], feats[8:16]], axis=1).astype(BF)
    for x in range(32):
        pay_ref[x] = pay
    fown_ref[...] = jnp.concatenate([feats, jnp.zeros((S, 64), F32)], axis=1).astype(BF)


def split_loss(loss):
    high = loss.astype(BF).astype(F32)
    mid = (loss - high).astype(BF).astype(F32)
    return high, mid, loss - high - mid


def tail_kernel(
    counts, position, g, wd1, wd2, wd3, targets, fown, gf_ref, mix_ref, small_ref, padded_ref
):
    ends = []
    for k in range(32):
        ends.append(counts[k] + (ends[-1] if k else 0))
    by_row = lax.broadcasted_iota(jnp.int32, (S, S), 0)
    by_col = lax.broadcasted_iota(jnp.int32, (S, S), 1)
    row_owner = jnp.zeros((S, S), jnp.int32)
    col_owner = jnp.zeros((S, S), jnp.int32)
    for end in ends:
        row_owner = row_owner + jnp.where(by_row >= end, 1, 0)
        col_owner = col_owner + jnp.where(by_col >= end, 1, 0)
    alike = jnp.where(row_owner == col_owner, 1.0, 0.0)
    same = alike / jnp.sum(alike, axis=1, keepdims=True)

    low = lane_ids((8, LANES)) < 64
    pairs = []
    for p in range(16):
        ga, gb = g[2 * p].astype(F32), g[2 * p + 1].astype(F32)
        lo = jnp.where(low, ga, pltpu.roll(gb, 64, 1))
        hi = jnp.where(low, pltpu.roll(ga, 64, 1), gb)
        pairs.append(jnp.concatenate([lo, hi], axis=0).astype(BF))
    feats = jnp.concatenate(pairs, axis=1)
    dense1 = mm(feats, wd1[...])
    centred = dense1 - 0.5 * mm_exact(same, dense1)
    t1 = jnp.tanh(centred)
    out1 = leaky(centred, t1).astype(BF)

    w2 = jnp.concatenate([wd2[...], jnp.zeros((64, LANES), BF)], axis=0)
    padded_ref[...] = jnp.zeros((LANES, LANES), F32)
    padded_ref[64:68, 0:64] = wd3[...].astype(F32)
    w3 = padded_ref[...].astype(BF)
    padded_ref[...] = jnp.zeros((LANES, LANES), F32)
    padded_ref[64:68, 0:S] = targets[...]
    goal = jnp.transpose(padded_ref[...], (1, 0))[0:S]

    dense2 = mm(out1, w2, NT)
    t2 = jnp.tanh(dense2)
    out2 = leaky(dense2, t2).astype(BF)
    diff = mm(out2, w3, NT) - goal
    loss = jnp.sum(jnp.sum(diff * diff, axis=1, keepdims=True), axis=0, keepdims=True) / 32.0
    gpred = (diff / 16.0).astype(BF)
    gdense2 = (mm(gpred, w3) * slope(dense2, t2)).astype(BF)
    gcentred = mm(gdense2, w2) * slope(centred, t1)
    gdense1 = (gcentred - 0.5 * mm_exact(same, gcentred)).astype(BF)
    here = position[0]
    after = jnp.minimum(here + 1, 31)
    for k, slab in enumerate((here, after)):
        rows = wd1[pl.ds(pl.multiple_of(slab * 64, 64), 64), :]
        gf_ref[k * 64 : (k + 1) * 64] = mm(rows, gdense1, NT)

    d1 = mm(fown[...], gdense1, TN)
    d2 = mm(gdense2, out1, TN)
    d3 = mm(gpred, out2, TN)[64:72]
    lanes = lane_ids((8, LANES))
    top = lax.broadcasted_iota(jnp.int32, (8, LANES), 0) == 0
    for k, piece in enumerate(split_loss(loss)):
        d3 = jnp.where(jnp.logical_and(top, lanes == 64 + k), piece, d3)
    small_ref[...] = d3
    for p in range(16):
        mix_ref[p * 8 : p * 8 + 4] = d1[p * 4 : p * 4 + 4]
        mix_ref[p * 8 + 4 : p * 8 + 8] = d2[p * 4 : p * 4 + 4]


def tap_sums(r_ref, rh_ref):
    group = lax.shift_right_logical(lane_ids((12, LANES)), 5)
    sums = [jnp.zeros((12, LANES), F32) for _ in range(9)]

    def add(rows, places):
        for g, a, b in places:
            if 0 <= a < 3 and 0 <= b < 3:
                sums[a * 3 + b] = sums[a * 3 + b] + jnp.where(group == g, rows, 0.0)

    for y in range(4):
        for x in range(4):
            add(
                r_ref[pl.ds(x * 4 + y, 12, stride=16), :],
                [(2 * i + j, x - 2 * i + 1, y - 2 * j + 1) for i in range(2) for j in range(2)],
            )
        add(rh_ref[pl.ds(y, 12, stride=4), :], [(j, 0, y - 2 * j + 1) for j in range(2)])
    out = []
    for total in sums:
        total = total + pltpu.roll(total, 64, 1)
        out.append(total + pltpu.roll(total, 32, 1))
    return out


def back_kernel(
    gf_ref, mix, small, first_ref, s1c, block, slope2, next2, near, out_ref,
    g_ref, h_ref, w_ref, r_ref, rh_ref,
):
    x4, a1c = parts(first_ref, *OWN)
    gf = gf_ref[...].astype(BF).astype(F32) * (1.0 / 128.0)
    for q in range(4):
        cols = slice(q * CHUNK, (q + 1) * CHUNK)
        spread = jnp.concatenate(
            [jnp.broadcast_to(gf[:, 4 * q + n : 4 * q + n + 1], (128, LANES)) for n in range(4)],
            axis=1,
        )
        go = spread[0:64] * slope2[:, cols].astype(F32)
        gn = spread[64:128] * next2[:, cols].astype(F32)
        g_ref[0:64, cols] = go.astype(BF)
        g_ref[64:128, cols] = gn.astype(BF)
        g_ref[128:192, cols] = shift_down(go).astype(BF)
        g_ref[192:256, cols] = shift_down(gn).astype(BF)
        gact = mm(block[...], g_ref[:, cols])
        s1b = parts(near, *NEAR)[2]
        for s in range(2):
            for i, s1 in enumerate((s1b, s1c)):
                r = (2 * s + i) * 64
                h_ref[s, i * 64 : (i + 1) * 64, cols] = (
                    gact[r : r + 64] * s1[s * 64 : (s + 1) * 64, cols].astype(F32)
                ).astype(BF)
    xh, a1b, _ = parts(near, *NEAR)
    w_ref[0:192] = mm(a1c[...], g_ref[0:128, :], NT)
    a1 = mm(a1b[...], g_ref[0:64, :], NT)
    w_ref[192:288] = jnp.concatenate([a1[0:96], a1[96:192]], axis=1)
    r_ref[...] = mm(x4[0:192, :], h_ref[0], NT) + mm(x4[128:320, :], h_ref[1], NT)
    rh_ref[...] = mm(xh[0:48, :], h_ref[0], NT) + mm(xh[32:80, :], h_ref[1], NT)
    sums = tap_sums(r_ref, rh_ref)
    group = lax.shift_right_logical(lane_ids((12, LANES)), 5)
    w_ref[288:384] = jnp.zeros((96, LANES), F32)
    for k in range(3):
        packed = sums[4 * k]
        for n in range(1, 4):
            if 4 * k + n < 9:
                packed = jnp.where(group == n, sums[4 * k + n], packed)
        w_ref[288 + 16 * k : 300 + 16 * k] = packed
    zero = jnp.zeros((8, LANES), F32)
    for p in range(16):
        out_ref[p] = jnp.concatenate(
            [w_ref[p * PART : (p + 1) * PART], small[...], mix[p * 8 : (p + 1) * 8], zero], axis=0
        ).astype(BF)


def low_half(a, b):
    rows = lax.broadcasted_iota(jnp.int32, (8, LANES), 0)
    return jnp.where(rows < 4, a, pltpu.roll(b, 4, 0))


def high_half(a, b):
    rows = lax.broadcasted_iota(jnp.int32, (8, LANES), 0)
    return jnp.where(rows < 4, pltpu.roll(a, 4, 0), b)


def group_kernel(got, out_ref, d2_ref, d3_ref, loss_ref):
    even, odd = got[0].astype(F32), got[1].astype(F32)
    for k in range(1, 8):
        even, odd = even + got[2 * k].astype(F32), odd + got[2 * k + 1].astype(F32)
    total = even[0:PART] + odd[0:PART]
    d1 = low_half(even[32:40], odd[32:40])
    pay = jnp.concatenate([total, d1], axis=0).astype(BF)
    for k in range(16):
        out_ref[k] = pay
    d2_ref[...] = pltpu.roll(even[32:40], 4, 0)
    small = even[PART:32]
    d3_ref[...] = small[0:4, 0:64]
    lanes = lane_ids((8, LANES))
    rows = lax.broadcasted_iota(jnp.int32, (8, LANES), 0)
    held = jnp.logical_and(jnp.logical_and(lanes >= 64, lanes < 67), rows == 0)
    values = jnp.where(held, small, 0.0)
    loss_ref[...] = jnp.sum(jnp.sum(values, axis=1, keepdims=True), axis=0, keepdims=True)


def column_kernel(got, d2, out_ref):
    blocks = [got[k].astype(F32) for k in range(16)]
    total = blocks[0][0:PART]
    for b in blocks[1:]:
        total = total + b[0:PART]
    pay = jnp.concatenate([total, d2[...]] + [b[PART:32] for b in blocks], axis=0).astype(BF)
    for k in range(8):
        out_ref[k] = pay


def last_kernel(core, mine, other, gw1_ref, gw2_ref, gd1_ref, gd2_ref, w_ref):
    first = core[0] == 0
    for k in range(8):
        a, b = mine[k].astype(F32), other[k].astype(F32)
        low, high = jnp.where(first, a, b), jnp.where(first, b, a)
        w_ref[2 * k * PART : (2 * k + 1) * PART] = low[0:PART]
        w_ref[(2 * k + 1) * PART : (2 * k + 2) * PART] = high[0:PART]
        gd2_ref[k * 8 : (k + 1) * 8] = low_half(low[PART:32], high[PART:32])
        for q in range(16):
            at = 32 + 8 * q
            lo, hi = low[at : at + 8], high[at : at + 8]
            gd1_ref[pl.ds(k * 256 + 2 * q, 8, stride=32), :] = low_half(lo, hi)
            gd1_ref[pl.ds(k * 256 + 2 * q + 1, 8, stride=32), :] = high_half(lo, hi)
    for a in range(3):
        for e in range(3):
            gw2_ref[a, 0, e] = jnp.zeros((32, 64), F32)
            for b in (1, 2):
                at = e * 64 + (b - 1) * 32
                right = a == 0
                if a == 1:
                    right = at >= 96
                    at = 192 + at % 96
                block = w_ref[at : at + 32]
                if right:
                    block = pltpu.roll(block, 64, 1)
                gw2_ref[a, b, e] = block[:, 0:64]
    for a in range(3):
        for b in range(3):
            k, n = divmod(a * 3 + b, 4)
            packed = w_ref[288 + 16 * k : 304 + 16 * k]
            if n:
                packed = pltpu.roll(packed, LANES - 32 * n, 1)
            for e in range(3):
                gw1_ref[a, b, e] = packed[4 * e : 4 * e + 4, 0:32]


def local(volumes, targets, counts, w_conv1, w_conv2, w_dense1, w_dense2, w_dense3):
    core = lax.axis_index("core").astype(jnp.int32).reshape(1)
    position = lax.axis_index(SLABS).astype(jnp.int32).reshape(1)
    forward = [(i, i + 1) for i in range(31)]
    backward = [(i + 1, i) for i in range(31)]
    swap = [(0, 1), (1, 0)]
    split = jnp.asarray(split_matrix(), BF)
    own, rim = (jnp.asarray(m, BF) for m in band_matrices())
    w1 = jnp.swapaxes(w_conv1, 3, 4).reshape(27, 4, 32)
    w2 = jnp.swapaxes(w_conv2, 3, 4)

    halo = lax.ppermute(volumes[:, :, 3], SLABS, forward)
    held_own, held_slope, away = call(
        first_kernel,
        [((sum(OWN), WIDE), BF), ((128, WIDE), BF), ((64, WIDE), BF)],
        (volumes, w1, w2),
        flops=10**9,
    )
    got = lax.ppermute(away, SLABS, forward)
    held_near, part, wd1, block = call(
        second_kernel,
        [
            ((sum(NEAR), WIDE), BF), ((64, WIDE), F32), ((2048, LANES), BF),
            ((256, 256), BF),
        ],
        (
            halo, split, w1, own, rim, w2, held_own, w_dense1,
        ),
        scratch=[pltpu.VMEM((2048, LANES), F32)],
        flops=2 * 10**9,
    )
    slope2, pay, fown = call(
        third_kernel,
        [((64, WIDE), BF), ((32, 8, LANES), BF), ((S, LANES), BF)],
        (part, got),
        flops=10**8,
    )
    gathered = lax.all_to_all(pay, SLABS, 0, 0, tiled=True)
    next2 = lax.ppermute(slope2, SLABS, backward)
    gf, mix, small = call(
        tail_kernel,
        [((LANES, S), F32), ((LANES, LANES), F32), ((8, LANES), F32)],
        (gathered, wd1, w_dense2.T, w_dense3.T, targets.T, fown),
        scalars=(counts, position),
        scratch=[pltpu.VMEM((LANES, LANES), F32)],
        flops=2000000000,
    )
    (scattered,) = call(
        back_kernel,
        [((16, 48, LANES), BF)],
        (gf, mix, small, held_own, held_slope, block, slope2, next2, held_near),
        scratch=[
            pltpu.VMEM((256, WIDE), BF), pltpu.VMEM((2, 128, WIDE), BF),
            pltpu.VMEM((16 * PART, LANES), F32), pltpu.VMEM((192, LANES), F32),
            pltpu.VMEM((48, LANES), F32),
        ],
        flops=2 * 10**9,
    )
    over_group = lax.all_to_all(scattered, (*DP, "core"), 0, 0, tiled=True)
    to_column, d2, d3, loss = call(
        group_kernel,
        [((16, 32, LANES), BF), ((8, LANES), F32), ((4, 64), F32), ((1, 1), F32)],
        (over_group,),
    )
    over_column = lax.all_to_all(to_column, COLUMN, 0, 0, tiled=True)
    (back,) = call(
        column_kernel, [((8, 160, LANES), BF)], (over_column, d2)
    )
    summed = lax.all_to_all(back, DP, 0, 0, tiled=True)
    other = lax.ppermute(summed, "core", swap)
    gw1, gw2, gd1, gd2 = call(
        last_kernel,
        [
            ((3, 3, 3, 4, 32), F32), ((3, 3, 3, 32, 64), F32),
            ((2048, LANES), F32), ((64, LANES), F32),
        ],
        (summed, other),
        scalars=(core,),
        scratch=[pltpu.VMEM((16 * PART, LANES), F32)],
    )
    return (
        loss.reshape(()), jnp.swapaxes(gw1, 3, 4), jnp.swapaxes(gw2, 3, 4), gd1, gd2.T, d3.T,
    )


def solution(mesh):
    fine = Mesh(mesh.devices.reshape(4, 2, 2, 8, 2), ("x", "yl", "yh", "z", "core"))
    placed = (P(DP, None, SLABS, None, None), P(DP, None), P(), P(), P(), P(), P(), P())
    return jax.shard_map(
        local, mesh=fine, in_specs=placed, out_specs=(P(), P(), P(), P(), P(), P()), check_vma=False
    )
```

```python
import functools

import jax
import jax.numpy as jnp
import numpy as np
from jax import lax
from jax.experimental import pallas as pl
from jax.experimental.pallas import tpu as pltpu
from jax.sharding import Mesh
from jax.sharding import PartitionSpec as P

BF = jnp.bfloat16
F32 = jnp.float32
SLABS = ("yh", "z", "core")
DP = ("x", "yl")
COLUMN = ("yh", "z")
S = 16
LANES = 128
WIDE = S * LANES
CHUNK = 512
PART = 24
SMALL = 16 * 1024 * 1024

NN = (((1,), (0,)), ((), ()))
NT = (((1,), (1,)), ((), ()))
TN = (((0,), (0,)), ((), ()))


def mm(a, b, dims=NN):
    return lax.dot_general(a, b, dims, preferred_element_type=F32)


def mm_exact(a, b):
    return lax.dot_general(
        a, b, NN, preferred_element_type=F32, precision=lax.Precision.HIGHEST
    )


def leaky(v, t):
    return v * (0.65 + 0.35 * t)


def slope(v, t):
    return 0.65 + 0.35 * t + 0.35 * v * (1.0 - t * t)


def lane_ids(shape):
    return lax.broadcasted_iota(jnp.int32, shape, len(shape) - 1)


def shift_up(x):
    parts = []
    for k in range(x.shape[1] // LANES):
        p = pltpu.roll(x[:, k * LANES : (k + 1) * LANES], 1, 1)
        parts.append(jnp.where(lane_ids(p.shape) == 0, 0.0, p))
    return jnp.concatenate(parts, axis=1)


def shift_down(x):
    parts = []
    for k in range(x.shape[1] // LANES):
        p = pltpu.roll(x[:, k * LANES : (k + 1) * LANES], LANES - 1, 1)
        parts.append(jnp.where(lane_ids(p.shape) == LANES - 1, 0.0, p))
    return jnp.concatenate(parts, axis=1)


def call(kernel, outs, args, scalars=(), scratch=(), vmem=SMALL, flops=10**8):
    size = sum(int(np.prod(s)) * jnp.dtype(d).itemsize for s, d in outs)
    return pl.pallas_call(
        kernel,
        out_shape=[jax.ShapeDtypeStruct(s, d) for s, d in outs],
        in_specs=[pl.BlockSpec(memory_space=pltpu.SMEM)] * len(scalars)
        + [pl.BlockSpec(memory_space=pltpu.VMEM)] * len(args),
        out_specs=[pl.BlockSpec(memory_space=pltpu.VMEM)] * len(outs),
        scratch_shapes=list(scratch),
        compiler_params=pltpu.CompilerParams(vmem_limit_bytes=vmem),
        cost_estimate=pl.CostEstimate(flops=flops, bytes_accessed=size, transcendentals=0),
    )(*scalars, *args)


def parts(ref, *heights):
    out, at = [], 0
    for h in heights:
        out.append(ref.at[at : at + h])
        at += h
    return out


def bands(taps, ref, *index):
    return jnp.concatenate([mm(taps, ref[(*index, j)], TN).astype(BF) for j in range(2)], axis=0)


def band_here(i, j, planes):
    row = lax.broadcasted_iota(jnp.int32, (108, 1), 0)
    tap = lax.shift_right_logical(row, 2)
    third = lax.shift_right_logical(tap * 43, 7)
    a = lax.shift_right_logical(third * 43, 7)
    e, b = tap - 3 * third, third - 3 * a
    row_key = (e * 4 + jnp.bitwise_and(row, 3)) * 64 + a * 8 + b
    col = lax.broadcasted_iota(jnp.int32, (1, 48 * planes), 1)
    y = jnp.bitwise_and(col, 3) - 2 * j + 1
    if planes == 4:
        x = jnp.bitwise_and(lax.shift_right_logical(col, 2), 3) - 2 * i + 1
        col_key = lax.shift_right_logical(col, 4) * 64 + x * 8 + y
    else:
        col_key = lax.shift_right_logical(col, 2) * 64 + y
    return jnp.where(row_key == col_key, 1.0, 0.0).astype(BF)


def store_plane(h, s, cols, a1_ref, slope_ref):
    t = jnp.tanh(h)
    act = leaky(h, t)
    slope_ref[s * 64 : (s + 1) * 64, cols] = slope(h, t).astype(BF)
    if s == 0:
        a1_ref[64:128, cols] = act.astype(BF)
    else:
        a1_ref[128:192, cols] = act.astype(BF)
        a1_ref[0:64, cols] = shift_up(act).astype(BF)


def taps_of(w2_ref, a):
    return jnp.concatenate([w2_ref[a, b, e] for e in range(3) for b in (1, 2)], axis=0)


def bands(taps, ref, *index):
    return jnp.concatenate([mm(taps, ref[(*index, j)], TN).astype(BF) for j in range(2)], axis=0)


OWN = (320, 192)
NEAR = (80, 192, 128, 128)


def separate(rows, split, out_ref, height, first, many):
    d = mm(rows, split[...])
    for k in range(5):
        for n in range(many):
            at = (first + n) * LANES
            out_ref[k * height : (k + 1) * height, at : at + LANES] = d[
                n * height : (n + 1) * height, k * LANES : (k + 1) * LANES
            ].astype(BF)


def matrices_kernel(split_ref, own_ref, rim_ref):
    z = lax.broadcasted_iota(jnp.int32, (512, LANES), 0)
    m = lax.broadcasted_iota(jnp.int32, (512, LANES), 1)
    for k in range(5):
        split_ref[:, k * LANES : (k + 1) * LANES] = jnp.where(z - 4 * m == k - 1, 1.0, 0.0).astype(BF)
    for j in range(2):
        for i in range(2):
            own_ref[i, j] = band_here(i, j, 4)
        rim_ref[j] = band_here(0, j, 1)


def first_kernel(v, w1, w2, split, own, out_ref, slope_ref, away_ref):
    x4_ref, a1_ref = parts(out_ref, *OWN)
    w = bands(w1[...].reshape(108, 32), own, 1)
    w2a = taps_of(w2, 0)
    for q in range(4):
        rows = jnp.concatenate([v[4 * q + n].reshape(64, 512) for n in range(4)], axis=0)
        separate(rows, split, x4_ref, 64, 4 * q, 4)
        cols = slice(q * CHUNK, (q + 1) * CHUNK)
        for s in range(2):
            h = mm(w, x4_ref[s * 128 : s * 128 + 192, cols])
            store_plane(h, s, cols, a1_ref, slope_ref)
        away_ref[:, cols] = mm(w2a, a1_ref[:, cols], TN).astype(BF)


def second_kernel(
    halo, split, w1, own, rim, w2, first_ref, s1c, out_ref, part_ref, back_ref
):
    x4, a1c = parts(first_ref, *OWN)
    xh_ref, a1_ref, slope_ref, slope_c_ref = parts(out_ref, *NEAR)
    slope_c_ref[...] = s1c[...]
    taps = w1[...].reshape(108, 32)
    w, wh = bands(taps, own, 0), bands(taps, rim)
    rows = jnp.concatenate([halo[n].reshape(16, 512) for n in range(S)], axis=0)
    separate(rows, split, xh_ref, 16, 0, S)
    taps_b, taps_c = taps_of(w2, 1), taps_of(w2, 2)
    for q in range(4):
        cols = slice(q * CHUNK, (q + 1) * CHUNK)
        for s in range(2):
            h = mm(w, x4[s * 128 : s * 128 + 192, cols]) + mm(
                wh, xh_ref[s * 32 : s * 32 + 48, cols]
            )
            store_plane(h, s, cols, a1_ref, slope_ref)
        part = mm(taps_b, a1_ref[:, cols], TN) + mm(taps_c, a1c[:, cols], TN)
        part_ref[:, cols] = part
        back_ref[:, cols] = part.astype(BF)


def between_kernel(part, away, wd1, w2, next2_ref, wd1_ref, block_ref, wide_ref):
    for q in range(4):
        cols = slice(q * CHUNK, (q + 1) * CHUNK)
        h2 = part[:, cols].astype(F32) + away[:, cols].astype(F32)
        next2_ref[:, cols] = slope(h2, jnp.tanh(h2)).astype(BF)

    def tap(a, e):
        return jnp.concatenate([w2[a, 1, e], w2[a, 2, e]], axis=0)

    zero = jnp.zeros((64, 64), BF)
    for k, row in enumerate(
        (
            (tap(1, 1), zero, zero, zero),
            (tap(2, 1), tap(0, 1), zero, zero),
            (tap(1, 2), zero, tap(1, 0), zero),
            (tap(2, 2), tap(0, 2), tap(2, 0), tap(0, 0)),
        )
    ):
        block_ref[k * 64 : (k + 1) * 64] = jnp.concatenate(row, axis=1)
    wide_ref[...] = wd1[...].astype(F32)
    for x in range(32):
        wd1_ref[x * 64 : (x + 1) * 64] = wide_ref[pl.ds(x, 64, stride=32), :].astype(BF)


def third_kernel(part, got, slope2_ref, pay_ref, fown_ref):
    total = jnp.zeros((S, 64), F32)
    for q in range(4):
        cols = slice(q * CHUNK, (q + 1) * CHUNK)
        h2 = part[:, cols] + got[:, cols].astype(F32)
        t = jnp.tanh(h2)
        act2 = leaky(h2, t).astype(BF)
        slope2_ref[:, cols] = slope(h2, t).astype(BF)
        rows = lax.broadcasted_iota(jnp.int32, (S, CHUNK), 0)
        owner = lax.shift_right_logical(lane_ids((S, CHUNK)), 7) + 4 * q
        pick = jnp.where(rows == owner, 1.0, 0.0).astype(BF)
        total = total + mm(pick, act2, NT)
    feats = total * (1.0 / 128.0)
    pay = jnp.concatenate([feats[0:8], feats[8:16]], axis=1).astype(BF)
    for x in range(32):
        pay_ref[x] = pay
    fown_ref[...] = jnp.concatenate([feats, jnp.zeros((S, 64), F32)], axis=1).astype(BF)


def split_loss(loss):
    high = loss.astype(BF).astype(F32)
    mid = (loss - high).astype(BF).astype(F32)
    return high, mid, loss - high - mid


def tail_kernel(
    counts, position, g, wd1, wd2, wd3, targets, fown, gf_ref, mix_ref, small_ref, padded_ref
):
    ends = []
    for k in range(32):
        ends.append(counts[k] + (ends[-1] if k else 0))
    by_row = lax.broadcasted_iota(jnp.int32, (S, S), 0)
    by_col = lax.broadcasted_iota(jnp.int32, (S, S), 1)
    row_owner = jnp.zeros((S, S), jnp.int32)
    col_owner = jnp.zeros((S, S), jnp.int32)
    for end in ends:
        row_owner = row_owner + jnp.where(by_row >= end, 1, 0)
        col_owner = col_owner + jnp.where(by_col >= end, 1, 0)
    alike = jnp.where(row_owner == col_owner, 1.0, 0.0)
    same = alike / jnp.sum(alike, axis=1, keepdims=True)

    low = lane_ids((8, LANES)) < 64
    pairs = []
    for p in range(16):
        ga, gb = g[2 * p].astype(F32), g[2 * p + 1].astype(F32)
        lo = jnp.where(low, ga, pltpu.roll(gb, 64, 1))
        hi = jnp.where(low, pltpu.roll(ga, 64, 1), gb)
        pairs.append(jnp.concatenate([lo, hi], axis=0).astype(BF))
    feats = jnp.concatenate(pairs, axis=1)
    dense1 = mm(feats, wd1[...])
    centred = dense1 - 0.5 * mm_exact(same, dense1)
    t1 = jnp.tanh(centred)
    out1 = leaky(centred, t1).astype(BF)

    w2 = jnp.concatenate([wd2[...], jnp.zeros((64, LANES), BF)], axis=0)
    padded_ref[...] = jnp.zeros((LANES, LANES), F32)
    padded_ref[64:68, 0:64] = wd3[...].astype(F32)
    w3 = padded_ref[...].astype(BF)
    padded_ref[...] = jnp.zeros((LANES, LANES), F32)
    padded_ref[64:68, 0:S] = targets[...]
    goal = jnp.transpose(padded_ref[...], (1, 0))[0:S]

    dense2 = mm(out1, w2, NT)
    t2 = jnp.tanh(dense2)
    out2 = leaky(dense2, t2).astype(BF)
    diff = mm(out2, w3, NT) - goal
    loss = jnp.sum(jnp.sum(diff * diff, axis=1, keepdims=True), axis=0, keepdims=True) / 32.0
    gpred = (diff / 16.0).astype(BF)
    gdense2 = (mm(gpred, w3) * slope(dense2, t2)).astype(BF)
    gcentred = mm(gdense2, w2) * slope(centred, t1)
    gdense1 = (gcentred - 0.5 * mm_exact(same, gcentred)).astype(BF)
    here = position[0]
    after = jnp.minimum(here + 1, 31)
    for k, slab in enumerate((here, after)):
        rows = wd1[pl.ds(pl.multiple_of(slab * 64, 64), 64), :]
        gf_ref[k * 64 : (k + 1) * 64] = mm(rows, gdense1, NT)
    gf_ref[64:128] = jnp.where(here < 31, gf_ref[64:128], 0.0)

    d1 = mm(fown[...], gdense1, TN)
    d2 = mm(gdense2, out1, TN)
    d3 = mm(gpred, out2, TN)[64:72]
    lanes = lane_ids((8, LANES))
    top = lax.broadcasted_iota(jnp.int32, (8, LANES), 0) == 0
    for k, piece in enumerate(split_loss(loss)):
        d3 = jnp.where(jnp.logical_and(top, lanes == 64 + k), piece, d3)
    small_ref[...] = d3
    for p in range(16):
        mix_ref[p * 8 : p * 8 + 4] = d1[p * 4 : p * 4 + 4]
        mix_ref[p * 8 + 4 : p * 8 + 8] = d2[p * 4 : p * 4 + 4]


def tap_sums(r_ref, rh_ref):
    group = lax.shift_right_logical(lane_ids((12, LANES)), 5)
    sums = [jnp.zeros((12, LANES), F32) for _ in range(9)]

    def add(rows, places):
        for g, a, b in places:
            if 0 <= a < 3 and 0 <= b < 3:
                sums[a * 3 + b] = sums[a * 3 + b] + jnp.where(group == g, rows, 0.0)

    for y in range(4):
        for x in range(4):
            add(
                r_ref[pl.ds(x * 4 + y, 12, stride=16), :],
                [(2 * i + j, x - 2 * i + 1, y - 2 * j + 1) for i in range(2) for j in range(2)],
            )
        add(rh_ref[pl.ds(y, 12, stride=4), :], [(j, 0, y - 2 * j + 1) for j in range(2)])
    out = []
    for total in sums:
        total = total + pltpu.roll(total, 64, 1)
        out.append(total + pltpu.roll(total, 32, 1))
    return out


def back_kernel(
    gf_ref, mix, small, first_ref, block, slope2, next2, near, out_ref,
    g_ref, h_ref, w_ref, r_ref, rh_ref,
):
    x4, a1c = parts(first_ref, *OWN)
    gf = gf_ref[...].astype(BF).astype(F32) * (1.0 / 128.0)
    for q in range(4):
        cols = slice(q * CHUNK, (q + 1) * CHUNK)
        spread = jnp.concatenate(
            [jnp.broadcast_to(gf[:, 4 * q + n : 4 * q + n + 1], (128, LANES)) for n in range(4)],
            axis=1,
        )
        go = spread[0:64] * slope2[:, cols].astype(F32)
        gn = spread[64:128] * next2[:, cols].astype(F32)
        g_ref[0:64, cols] = go.astype(BF)
        g_ref[64:128, cols] = gn.astype(BF)
        g_ref[128:192, cols] = shift_down(go).astype(BF)
        g_ref[192:256, cols] = shift_down(gn).astype(BF)
        gact = mm(block[...], g_ref[:, cols])
        s1b, s1c = parts(near, *NEAR)[2:]
        for s in range(2):
            for i, s1 in enumerate((s1b, s1c)):
                r = (2 * s + i) * 64
                h_ref[s, i * 64 : (i + 1) * 64, cols] = (
                    gact[r : r + 64] * s1[s * 64 : (s + 1) * 64, cols].astype(F32)
                ).astype(BF)
    xh, a1b = parts(near, *NEAR)[:2]
    w_ref[0:192] = mm(a1c[...], g_ref[0:128, :], NT)
    a1 = mm(a1b[...], g_ref[0:64, :], NT)
    w_ref[192:288] = jnp.concatenate([a1[0:96], a1[96:192]], axis=1)
    r_ref[...] = mm(x4[0:192, :], h_ref[0], NT) + mm(x4[128:320, :], h_ref[1], NT)
    rh_ref[...] = mm(xh[0:48, :], h_ref[0], NT) + mm(xh[32:80, :], h_ref[1], NT)
    sums = tap_sums(r_ref, rh_ref)
    group = lax.shift_right_logical(lane_ids((12, LANES)), 5)
    w_ref[288:384] = jnp.zeros((96, LANES), F32)
    for k in range(3):
        packed = sums[4 * k]
        for n in range(1, 4):
            if 4 * k + n < 9:
                packed = jnp.where(group == n, sums[4 * k + n], packed)
        w_ref[288 + 16 * k : 300 + 16 * k] = packed
    zero = jnp.zeros((8, LANES), F32)
    for p in range(16):
        out_ref[p] = jnp.concatenate(
            [w_ref[p * PART : (p + 1) * PART], small[...], mix[p * 8 : (p + 1) * 8], zero], axis=0
        ).astype(BF)


def low_half(a, b):
    rows = lax.broadcasted_iota(jnp.int32, (8, LANES), 0)
    return jnp.where(rows < 4, a, pltpu.roll(b, 4, 0))


def high_half(a, b):
    rows = lax.broadcasted_iota(jnp.int32, (8, LANES), 0)
    return jnp.where(rows < 4, pltpu.roll(a, 4, 0), b)


def group_kernel(got, out_ref, d2_ref, d3_ref, loss_ref):
    even, odd = got[0].astype(F32), got[1].astype(F32)
    for k in range(1, 8):
        even, odd = even + got[2 * k].astype(F32), odd + got[2 * k + 1].astype(F32)
    total = even[0:PART] + odd[0:PART]
    d1 = low_half(even[32:40], odd[32:40])
    pay = jnp.concatenate([total, d1], axis=0).astype(BF)
    for k in range(16):
        out_ref[k] = pay
    d2_ref[...] = pltpu.roll(even[32:40], 4, 0)
    small = even[PART:32]
    d3_ref[...] = small[0:4, 0:64]
    lanes = lane_ids((8, LANES))
    rows = lax.broadcasted_iota(jnp.int32, (8, LANES), 0)
    held = jnp.logical_and(jnp.logical_and(lanes >= 64, lanes < 67), rows == 0)
    values = jnp.where(held, small, 0.0)
    loss_ref[...] = jnp.sum(jnp.sum(values, axis=1, keepdims=True), axis=0, keepdims=True)


def column_kernel(got, d2, out_ref):
    blocks = [got[k].astype(F32) for k in range(16)]
    total = blocks[0][0:PART]
    for b in blocks[1:]:
        total = total + b[0:PART]
    pay = jnp.concatenate([total, d2[...]] + [b[PART:32] for b in blocks], axis=0).astype(BF)
    for k in range(8):
        out_ref[k] = pay


def last_kernel(core, mine, other, gw1_ref, gw2_ref, gd1_ref, gd2_ref, w_ref):
    first = core[0] == 0
    for k in range(8):
        a, b = mine[k].astype(F32), other[k].astype(F32)
        low, high = jnp.where(first, a, b), jnp.where(first, b, a)
        w_ref[2 * k * PART : (2 * k + 1) * PART] = low[0:PART]
        w_ref[(2 * k + 1) * PART : (2 * k + 2) * PART] = high[0:PART]
        gd2_ref[k * 8 : (k + 1) * 8] = low_half(low[PART:32], high[PART:32])
        for q in range(16):
            at = 32 + 8 * q
            lo, hi = low[at : at + 8], high[at : at + 8]
            gd1_ref[pl.ds(k * 256 + 2 * q, 8, stride=32), :] = low_half(lo, hi)
            gd1_ref[pl.ds(k * 256 + 2 * q + 1, 8, stride=32), :] = high_half(lo, hi)
    for a in range(3):
        for e in range(3):
            gw2_ref[a, 0, e] = jnp.zeros((32, 64), F32)
            for b in (1, 2):
                at = e * 64 + (b - 1) * 32
                right = a == 0
                if a == 1:
                    right = at >= 96
                    at = 192 + at % 96
                block = w_ref[at : at + 32]
                if right:
                    block = pltpu.roll(block, 64, 1)
                gw2_ref[a, b, e] = block[:, 0:64]
    for a in range(3):
        for b in range(3):
            k, n = divmod(a * 3 + b, 4)
            packed = w_ref[288 + 16 * k : 304 + 16 * k]
            if n:
                packed = pltpu.roll(packed, LANES - 32 * n, 1)
            for e in range(3):
                gw1_ref[a, b, e] = packed[4 * e : 4 * e + 4, 0:32]


def local(volumes, targets, counts, w_conv1, w_conv2, w_dense1, w_dense2, w_dense3):
    core = lax.axis_index("core").astype(jnp.int32).reshape(1)
    position = lax.axis_index(SLABS).astype(jnp.int32).reshape(1)
    forward = [(i, i + 1) for i in range(31)]
    backward = [(i + 1, i) for i in range(31)]
    swap = [(0, 1), (1, 0)]
    split, own, rim = call(
        matrices_kernel,
        [((512, 640), BF), ((2, 2, 108, 192), BF), ((2, 108, 48), BF)],
        (),
        flops=2 * 10**9,
    )
    w1 = jnp.swapaxes(w_conv1, 3, 4).reshape(27, 4, 32)
    w2 = jnp.swapaxes(w_conv2, 3, 4)

    halo = lax.ppermute(volumes[:, :, 3], SLABS, forward)
    held_own, held_slope, away = call(
        first_kernel,
        [((sum(OWN), WIDE), BF), ((128, WIDE), BF), ((64, WIDE), BF)],
        (volumes, w1, w2, split, own),
        flops=10**9,
    )
    got = lax.ppermute(away, SLABS, forward)
    held_near, part, part_back = call(
        second_kernel,
        [((sum(NEAR), WIDE), BF), ((64, WIDE), F32), ((64, WIDE), BF)],
        (halo, split, w1, own, rim, w2, held_own, held_slope),
        flops=2 * 10**9,
    )
    part_next = lax.ppermute(part_back, SLABS, backward)
    slope2, pay, fown = call(
        third_kernel,
        [((64, WIDE), BF), ((32, 8, LANES), BF), ((S, LANES), BF)],
        (part, got),
        flops=3 * 10**9,
    )
    gathered = lax.all_to_all(pay, SLABS, 0, 0, tiled=True)
    next2, wd1, block = call(
        between_kernel,
        [((64, WIDE), BF), ((2048, LANES), BF), ((256, 256), BF)],
        (part_next, away, w_dense1, w2),
        scratch=[pltpu.VMEM((2048, LANES), F32)],
        flops=10**8,
    )
    gf, mix, small = call(
        tail_kernel,
        [((LANES, S), F32), ((LANES, LANES), F32), ((8, LANES), F32)],
        (gathered, wd1, w_dense2.T, w_dense3.T, targets.T, fown),
        scalars=(counts, position),
        scratch=[pltpu.VMEM((LANES, LANES), F32)],
        flops=2000000000,
    )
    (scattered,) = call(
        back_kernel,
        [((16, 48, LANES), BF)],
        (gf, mix, small, held_own, block, slope2, next2, held_near),
        scratch=[
            pltpu.VMEM((256, WIDE), BF), pltpu.VMEM((2, 128, WIDE), BF),
            pltpu.VMEM((16 * PART, LANES), F32), pltpu.VMEM((192, LANES), F32),
            pltpu.VMEM((48, LANES), F32),
        ],
        flops=2 * 10**9,
    )
    over_group = lax.all_to_all(scattered, (*DP, "core"), 0, 0, tiled=True)
    to_column, d2, d3, loss = call(
        group_kernel,
        [((16, 32, LANES), BF), ((8, LANES), F32), ((4, 64), F32), ((1, 1), F32)],
        (over_group,),
    )
    over_column = lax.all_to_all(to_column, COLUMN, 0, 0, tiled=True)
    (back,) = call(
        column_kernel, [((8, 160, LANES), BF)], (over_column, d2)
    )
    summed = lax.all_to_all(back, DP, 0, 0, tiled=True)
    other = lax.ppermute(summed, "core", swap)
    gw1, gw2, gd1, gd2 = call(
        last_kernel,
        [
            ((3, 3, 3, 4, 32), F32), ((3, 3, 3, 32, 64), F32),
            ((2048, LANES), F32), ((64, LANES), F32),
        ],
        (summed, other),
        scalars=(core,),
        scratch=[pltpu.VMEM((16 * PART, LANES), F32)],
    )
    return (
        loss.reshape(()), jnp.swapaxes(gw1, 3, 4), jnp.swapaxes(gw2, 3, 4), gd1, gd2.T, d3.T,
    )


def solution(mesh):
    fine = Mesh(mesh.devices.reshape(4, 2, 2, 8, 2), ("x", "yl", "yh", "z", "core"))
    placed = (P(DP, None, SLABS, None, None), P(DP, None), P(), P(), P(), P(), P(), P())
    return jax.shard_map(
        local, mesh=fine, in_specs=placed, out_specs=(P(), P(), P(), P(), P(), P()), check_vma=False
    )
```

```python
import functools

import jax
import jax.numpy as jnp
import numpy as np
from jax import lax
from jax.experimental import pallas as pl
from jax.experimental.pallas import tpu as pltpu
from jax.sharding import Mesh
from jax.sharding import PartitionSpec as P

BF = jnp.bfloat16
F32 = jnp.float32
SLABS = ("yh", "z", "core")
DP = ("x", "yl")
COLUMN = ("yh", "z")
S = 16
LANES = 128
WIDE = S * LANES
CHUNK = 512
PART = 24
SMALL = 16 * 1024 * 1024

NN = (((1,), (0,)), ((), ()))
NT = (((1,), (1,)), ((), ()))
TN = (((0,), (0,)), ((), ()))


def mm(a, b, dims=NN):
    return lax.dot_general(a, b, dims, preferred_element_type=F32)


def three(x):
    high = x.astype(BF)
    rest = x - high.astype(F32)
    mid = rest.astype(BF)
    return high, mid, (rest - mid.astype(F32)).astype(BF)


def leaky(v, t):
    return v * (0.65 + 0.35 * t)


def slope(v, t):
    return 0.65 + 0.35 * t + 0.35 * v * (1.0 - t * t)


def lane_ids(shape):
    return lax.broadcasted_iota(jnp.int32, shape, len(shape) - 1)


def shift_up(x):
    parts = []
    for k in range(x.shape[1] // LANES):
        p = pltpu.roll(x[:, k * LANES : (k + 1) * LANES], 1, 1)
        parts.append(jnp.where(lane_ids(p.shape) == 0, 0.0, p))
    return jnp.concatenate(parts, axis=1)


def shift_down(x):
    parts = []
    for k in range(x.shape[1] // LANES):
        p = pltpu.roll(x[:, k * LANES : (k + 1) * LANES], LANES - 1, 1)
        parts.append(jnp.where(lane_ids(p.shape) == LANES - 1, 0.0, p))
    return jnp.concatenate(parts, axis=1)


def call(kernel, outs, args, scalars=(), scratch=(), vmem=SMALL, flops=10**8):
    size = sum(int(np.prod(s)) * jnp.dtype(d).itemsize for s, d in outs)
    return pl.pallas_call(
        kernel,
        out_shape=[jax.ShapeDtypeStruct(s, d) for s, d in outs],
        in_specs=[pl.BlockSpec(memory_space=pltpu.SMEM)] * len(scalars)
        + [pl.BlockSpec(memory_space=pltpu.VMEM)] * len(args),
        out_specs=[pl.BlockSpec(memory_space=pltpu.VMEM)] * len(outs),
        scratch_shapes=list(scratch),
        compiler_params=pltpu.CompilerParams(vmem_limit_bytes=vmem),
        cost_estimate=pl.CostEstimate(flops=flops, bytes_accessed=size, transcendentals=0),
    )(*scalars, *args)


def parts(ref, *heights):
    out, at = [], 0
    for h in heights:
        out.append(ref.at[at : at + h])
        at += h
    return out


def bands(taps, ref, *index):
    return jnp.concatenate([mm(taps, ref[(*index, j)], TN).astype(BF) for j in range(2)], axis=0)


def band_here(i, j, planes):
    row = lax.broadcasted_iota(jnp.int32, (108, 1), 0)
    tap = lax.shift_right_logical(row, 2)
    third = lax.shift_right_logical(tap * 43, 7)
    a = lax.shift_right_logical(third * 43, 7)
    e, b = tap - 3 * third, third - 3 * a
    row_key = (e * 4 + jnp.bitwise_and(row, 3)) * 64 + a * 8 + b
    col = lax.broadcasted_iota(jnp.int32, (1, 48 * planes), 1)
    y = jnp.bitwise_and(col, 3) - 2 * j + 1
    if planes == 4:
        x = jnp.bitwise_and(lax.shift_right_logical(col, 2), 3) - 2 * i + 1
        col_key = lax.shift_right_logical(col, 4) * 64 + x * 8 + y
    else:
        col_key = lax.shift_right_logical(col, 2) * 64 + y
    return jnp.where(row_key == col_key, 1.0, 0.0).astype(BF)


def store_plane(h, s, cols, a1_ref, slope_ref):
    t = jnp.tanh(h)
    act = leaky(h, t)
    slope_ref[s * 64 : (s + 1) * 64, cols] = slope(h, t).astype(BF)
    if s == 0:
        a1_ref[64:128, cols] = act.astype(BF)
    else:
        a1_ref[128:192, cols] = act.astype(BF)
        a1_ref[0:64, cols] = shift_up(act).astype(BF)


def taps_of(w2_ref, a):
    return jnp.concatenate([w2_ref[a, b, e] for e in range(3) for b in (1, 2)], axis=0)


def bands(taps, ref, *index):
    return jnp.concatenate([mm(taps, ref[(*index, j)], TN).astype(BF) for j in range(2)], axis=0)


OWN = (320, 192)
NEAR = (80, 192, 128, 128)


def separate(rows, split, out_ref, height, first, many):
    d = mm(rows, split[...])
    for k in range(5):
        for n in range(many):
            at = (first + n) * LANES
            out_ref[k * height : (k + 1) * height, at : at + LANES] = d[
                n * height : (n + 1) * height, k * LANES : (k + 1) * LANES
            ].astype(BF)


def matrices_kernel(split_ref, own_ref, rim_ref):
    z = lax.broadcasted_iota(jnp.int32, (512, LANES), 0)
    m = lax.broadcasted_iota(jnp.int32, (512, LANES), 1)
    for k in range(5):
        split_ref[:, k * LANES : (k + 1) * LANES] = jnp.where(z - 4 * m == k - 1, 1.0, 0.0).astype(BF)
    for j in range(2):
        for i in range(2):
            own_ref[i, j] = band_here(i, j, 4)
        rim_ref[j] = band_here(0, j, 1)


def first_kernel(v, w1, w2, split, own, out_ref, slope_ref, away_ref):
    x4_ref, a1_ref = parts(out_ref, *OWN)
    w = bands(w1[...].reshape(108, 32), own, 1)
    w2a = taps_of(w2, 0)
    for q in range(4):
        rows = jnp.concatenate([v[4 * q + n].reshape(64, 512) for n in range(4)], axis=0)
        separate(rows, split, x4_ref, 64, 4 * q, 4)
        cols = slice(q * CHUNK, (q + 1) * CHUNK)
        for s in range(2):
            h = mm(w, x4_ref[s * 128 : s * 128 + 192, cols])
            store_plane(h, s, cols, a1_ref, slope_ref)
        away_ref[:, cols] = mm(w2a, a1_ref[:, cols], TN).astype(BF)


def second_kernel(
    halo, split, w1, own, rim, w2, first_ref, s1c, out_ref, part_ref, back_ref
):
    x4, a1c = parts(first_ref, *OWN)
    xh_ref, a1_ref, slope_ref, slope_c_ref = parts(out_ref, *NEAR)
    slope_c_ref[...] = s1c[...]
    taps = w1[...].reshape(108, 32)
    w, wh = bands(taps, own, 0), bands(taps, rim)
    rows = jnp.concatenate([halo[n].reshape(16, 512) for n in range(S)], axis=0)
    separate(rows, split, xh_ref, 16, 0, S)
    taps_b, taps_c = taps_of(w2, 1), taps_of(w2, 2)
    for q in range(4):
        cols = slice(q * CHUNK, (q + 1) * CHUNK)
        for s in range(2):
            h = mm(w, x4[s * 128 : s * 128 + 192, cols]) + mm(
                wh, xh_ref[s * 32 : s * 32 + 48, cols]
            )
            store_plane(h, s, cols, a1_ref, slope_ref)
        part = mm(taps_b, a1_ref[:, cols], TN) + mm(taps_c, a1c[:, cols], TN)
        part_ref[:, cols] = part
        back_ref[:, cols] = part.astype(BF)


def between_kernel(part, away, wd1, w2, next2_ref, wd1_ref, block_ref, wide_ref):
    for q in range(4):
        cols = slice(q * CHUNK, (q + 1) * CHUNK)
        h2 = part[:, cols].astype(F32) + away[:, cols].astype(F32)
        next2_ref[:, cols] = slope(h2, jnp.tanh(h2)).astype(BF)

    def tap(a, e):
        return jnp.concatenate([w2[a, 1, e], w2[a, 2, e]], axis=0)

    zero = jnp.zeros((64, 64), BF)
    for k, row in enumerate(
        (
            (tap(1, 1), zero, zero, zero),
            (tap(2, 1), tap(0, 1), zero, zero),
            (tap(1, 2), zero, tap(1, 0), zero),
            (tap(2, 2), tap(0, 2), tap(2, 0), tap(0, 0)),
        )
    ):
        block_ref[k * 64 : (k + 1) * 64] = jnp.concatenate(row, axis=1)
    wide_ref[...] = wd1[...].astype(F32)
    for x in range(32):
        wd1_ref[x * 64 : (x + 1) * 64] = wide_ref[pl.ds(x, 64, stride=32), :].astype(BF)


def third_kernel(part, got, slope2_ref, pay_ref, fown_ref):
    total = jnp.zeros((S, 64), F32)
    for q in range(4):
        cols = slice(q * CHUNK, (q + 1) * CHUNK)
        h2 = part[:, cols] + got[:, cols].astype(F32)
        t = jnp.tanh(h2)
        act2 = leaky(h2, t).astype(BF)
        slope2_ref[:, cols] = slope(h2, t).astype(BF)
        rows = lax.broadcasted_iota(jnp.int32, (S, CHUNK), 0)
        owner = lax.shift_right_logical(lane_ids((S, CHUNK)), 7) + 4 * q
        pick = jnp.where(rows == owner, 1.0, 0.0).astype(BF)
        total = total + mm(pick, act2, NT)
    feats = total * (1.0 / 128.0)
    pay = jnp.concatenate([feats[0:8], feats[8:16]], axis=1).astype(BF)
    for x in range(32):
        pay_ref[x] = pay
    fown_ref[...] = jnp.concatenate([feats, jnp.zeros((S, 64), F32)], axis=1).astype(BF)


def tail_kernel(
    counts, position, g, wd1, wd2, wd3, targets, fown, gf_ref, mix_ref, small_ref, padded_ref
):
    ends = []
    for k in range(32):
        ends.append(counts[k] + (ends[-1] if k else 0))
    by_row = lax.broadcasted_iota(jnp.int32, (S, S), 0)
    by_col = lax.broadcasted_iota(jnp.int32, (S, S), 1)
    row_owner = jnp.zeros((S, S), jnp.int32)
    col_owner = jnp.zeros((S, S), jnp.int32)
    for end in ends:
        row_owner = row_owner + jnp.where(by_row >= end, 1, 0)
        col_owner = col_owner + jnp.where(by_col >= end, 1, 0)
    alike = jnp.where(row_owner == col_owner, 1.0, 0.0)
    same = (alike / jnp.sum(alike, axis=1, keepdims=True)).astype(BF)
    same = jnp.concatenate([same] * 3, axis=1)

    low = lane_ids((8, LANES)) < 64
    pairs = []
    for p in range(16):
        ga, gb = g[2 * p].astype(F32), g[2 * p + 1].astype(F32)
        lo = jnp.where(low, ga, pltpu.roll(gb, 64, 1))
        hi = jnp.where(low, pltpu.roll(ga, 64, 1), gb)
        pairs.append(jnp.concatenate([lo, hi], axis=0).astype(BF))
    feats = jnp.concatenate(pairs, axis=1)
    dense1 = mm(feats, wd1[...])
    centred = dense1 - 0.5 * mm(same, jnp.concatenate(three(dense1), axis=0))
    t1 = jnp.tanh(centred)
    out1 = leaky(centred, t1).astype(BF)

    w2 = jnp.concatenate([wd2[...], jnp.zeros((64, LANES), BF)], axis=0)
    padded_ref[...] = jnp.zeros((LANES, LANES), F32)
    padded_ref[64:68, 0:64] = wd3[...].astype(F32)
    w3 = padded_ref[...].astype(BF)
    padded_ref[...] = jnp.zeros((LANES, LANES), F32)
    padded_ref[64:68, 0:S] = targets[...]
    goal = jnp.transpose(padded_ref[...], (1, 0))[0:S]

    dense2 = mm(out1, w2, NT)
    t2 = jnp.tanh(dense2)
    out2 = leaky(dense2, t2).astype(BF)
    diff = mm(out2, w3, NT) - goal
    loss = jnp.sum(jnp.sum(diff * diff, axis=1, keepdims=True), axis=0, keepdims=True) / 32.0
    gpred = (diff / 16.0).astype(BF)
    gdense2 = (mm(gpred, w3) * slope(dense2, t2)).astype(BF)
    gcentred = mm(gdense2, w2) * slope(centred, t1)
    gdense1 = (gcentred - 0.5 * mm(same, jnp.concatenate(three(gcentred), axis=0))).astype(BF)
    here = position[0]
    after = jnp.minimum(here + 1, 31)
    for k, slab in enumerate((here, after)):
        rows = wd1[pl.ds(pl.multiple_of(slab * 64, 64), 64), :]
        gf_ref[k * 64 : (k + 1) * 64] = mm(rows, gdense1, NT)
    gf_ref[64:128] = jnp.where(here < 31, gf_ref[64:128], 0.0)

    d1 = mm(fown[...], gdense1, TN)
    d2 = mm(gdense2, out1, TN)
    d3 = mm(gpred, out2, TN)[64:72]
    lanes = lane_ids((8, LANES))
    top = lax.broadcasted_iota(jnp.int32, (8, LANES), 0) == 0
    for k, piece in enumerate(three(loss)):
        d3 = jnp.where(jnp.logical_and(top, lanes == 64 + k), piece.astype(F32), d3)
    small_ref[...] = d3
    for k in range(8):
        pair = d1[k * 8 : (k + 1) * 8], d2[k * 8 : (k + 1) * 8]
        mix_ref[k * 16 : k * 16 + 8] = low_half(*pair)
        mix_ref[k * 16 + 8 : k * 16 + 16] = high_half(*pair)


def tap_sums(r_ref, rh_ref):
    group = lax.shift_right_logical(lane_ids((12, LANES)), 5)
    sums = [jnp.zeros((12, LANES), F32) for _ in range(9)]

    def add(rows, places):
        for g, a, b in places:
            if 0 <= a < 3 and 0 <= b < 3:
                sums[a * 3 + b] = sums[a * 3 + b] + jnp.where(group == g, rows, 0.0)

    for y in range(4):
        for x in range(4):
            add(
                r_ref[pl.ds(x * 4 + y, 12, stride=16), :],
                [(2 * i + j, x - 2 * i + 1, y - 2 * j + 1) for i in range(2) for j in range(2)],
            )
        add(rh_ref[pl.ds(y, 12, stride=4), :], [(j, 0, y - 2 * j + 1) for j in range(2)])
    out = []
    for total in sums:
        total = total + pltpu.roll(total, 64, 1)
        out.append(total + pltpu.roll(total, 32, 1))
    return out


def back_kernel(
    gf_ref, mix, small, first_ref, block, slope2, next2, near, out_ref,
    g_ref, h_ref, w_ref, r_ref, rh_ref,
):
    x4, a1c = parts(first_ref, *OWN)
    gf = gf_ref[...].astype(BF).astype(F32) * (1.0 / 128.0)
    for q in range(4):
        cols = slice(q * CHUNK, (q + 1) * CHUNK)
        spread = jnp.concatenate(
            [jnp.broadcast_to(gf[:, 4 * q + n : 4 * q + n + 1], (128, LANES)) for n in range(4)],
            axis=1,
        )
        go = spread[0:64] * slope2[:, cols].astype(F32)
        gn = spread[64:128] * next2[:, cols].astype(F32)
        g_ref[0:64, cols] = go.astype(BF)
        g_ref[64:128, cols] = gn.astype(BF)
        g_ref[128:192, cols] = shift_down(go).astype(BF)
        g_ref[192:256, cols] = shift_down(gn).astype(BF)
        gact = mm(block[...], g_ref[:, cols])
        s1b, s1c = parts(near, *NEAR)[2:]
        for s in range(2):
            for i, s1 in enumerate((s1b, s1c)):
                r = (2 * s + i) * 64
                h_ref[s, i * 64 : (i + 1) * 64, cols] = (
                    gact[r : r + 64] * s1[s * 64 : (s + 1) * 64, cols].astype(F32)
                ).astype(BF)
    xh, a1b = parts(near, *NEAR)[:2]
    w_ref[0:192] = mm(a1c[...], g_ref[0:128, :], NT)
    a1 = mm(a1b[...], g_ref[0:64, :], NT)
    w_ref[192:288] = jnp.concatenate([a1[0:96], a1[96:192]], axis=1)
    r_ref[...] = mm(x4[0:192, :], h_ref[0], NT) + mm(x4[128:320, :], h_ref[1], NT)
    rh_ref[...] = mm(xh[0:48, :], h_ref[0], NT) + mm(xh[32:80, :], h_ref[1], NT)
    sums = tap_sums(r_ref, rh_ref)
    group = lax.shift_right_logical(lane_ids((12, LANES)), 5)
    w_ref[288:384] = jnp.zeros((96, LANES), F32)
    for k in range(3):
        packed = sums[4 * k]
        for n in range(1, 4):
            if 4 * k + n < 9:
                packed = jnp.where(group == n, sums[4 * k + n], packed)
        w_ref[288 + 16 * k : 300 + 16 * k] = packed
    zero = jnp.zeros((8, LANES), F32)
    for p in range(16):
        out_ref[p] = jnp.concatenate(
            [w_ref[p * PART : (p + 1) * PART], small[...], mix[p * 8 : (p + 1) * 8], zero], axis=0
        ).astype(BF)


def low_half(a, b):
    rows = lax.broadcasted_iota(jnp.int32, (8, LANES), 0)
    return jnp.where(rows < 4, a, pltpu.roll(b, 4, 0))


def high_half(a, b):
    rows = lax.broadcasted_iota(jnp.int32, (8, LANES), 0)
    return jnp.where(rows < 4, pltpu.roll(a, 4, 0), b)


def group_kernel(got, out_ref, d2_ref, d3_ref, loss_ref):
    even, odd = got[0].astype(F32), got[1].astype(F32)
    for k in range(1, 8):
        even, odd = even + got[2 * k].astype(F32), odd + got[2 * k + 1].astype(F32)
    total = even[0:PART] + odd[0:PART]
    d1 = low_half(even[32:40], odd[32:40])
    pay = jnp.concatenate([total, d1], axis=0).astype(BF)
    for k in range(16):
        out_ref[k] = pay
    d2_ref[...] = pltpu.roll(even[32:40], 4, 0)
    small = even[PART:32]
    d3_ref[...] = small[0:4, 0:64]
    lanes = lane_ids((8, LANES))
    rows = lax.broadcasted_iota(jnp.int32, (8, LANES), 0)
    held = jnp.logical_and(jnp.logical_and(lanes >= 64, lanes < 67), rows == 0)
    values = jnp.where(held, small, 0.0)
    loss_ref[...] = jnp.sum(jnp.sum(values, axis=1, keepdims=True), axis=0, keepdims=True)


def column_kernel(got, d2, out_ref):
    blocks = [got[k].astype(F32) for k in range(16)]
    total = blocks[0][0:PART]
    for b in blocks[1:]:
        total = total + b[0:PART]
    pay = jnp.concatenate([total, d2[...]] + [b[PART:32] for b in blocks], axis=0).astype(BF)
    for k in range(8):
        out_ref[k] = pay


def last_kernel(core, mine, other, gw1_ref, gw2_ref, gd1_ref, gd2_ref, w_ref, t_ref):
    first = core[0] == 0
    for k in range(8):
        for n, chunk in enumerate((mine, other)):
            t_ref[2 * k + n] = chunk[k, 32:160].astype(F32)
            base = k * 256 + jnp.bitwise_xor(core[0], n) * 128
            for r in range(4):
                at = pl.multiple_of(base + r * 32, 32)
                gd1_ref[pl.ds(at, 32), :] = t_ref[2 * k + n, pl.ds(r, 32, stride=4), :]
        a, b = mine[k, 0:32].astype(F32), other[k, 0:32].astype(F32)
        low, high = jnp.where(first, a, b), jnp.where(first, b, a)
        w_ref[2 * k * PART : (2 * k + 1) * PART] = low[0:PART]
        w_ref[(2 * k + 1) * PART : (2 * k + 2) * PART] = high[0:PART]
        gd2_ref[k * 8 : (k + 1) * 8] = low_half(low[PART:32], high[PART:32])
    for a in range(3):
        for e in range(3):
            gw2_ref[a, 0, e] = jnp.zeros((32, 64), F32)
            for b in (1, 2):
                at = e * 64 + (b - 1) * 32
                right = a == 0
                if a == 1:
                    right = at >= 96
                    at = 192 + at % 96
                block = w_ref[at : at + 32]
                if right:
                    block = pltpu.roll(block, 64, 1)
                gw2_ref[a, b, e] = block[:, 0:64]
    for a in range(3):
        for b in range(3):
            k, n = divmod(a * 3 + b, 4)
            packed = w_ref[288 + 16 * k : 304 + 16 * k]
            if n:
                packed = pltpu.roll(packed, LANES - 32 * n, 1)
            for e in range(3):
                gw1_ref[a, b, e] = packed[4 * e : 4 * e + 4, 0:32]


def local(volumes, targets, counts, w_conv1, w_conv2, w_dense1, w_dense2, w_dense3):
    core = lax.axis_index("core").astype(jnp.int32).reshape(1)
    position = lax.axis_index(SLABS).astype(jnp.int32).reshape(1)
    forward = [(i, i + 1) for i in range(31)]
    backward = [(i + 1, i) for i in range(31)]
    swap = [(0, 1), (1, 0)]
    split, own, rim = call(
        matrices_kernel,
        [((512, 640), BF), ((2, 2, 108, 192), BF), ((2, 108, 48), BF)],
        (),
        flops=2 * 10**9,
    )
    w1 = jnp.swapaxes(w_conv1, 3, 4).reshape(27, 4, 32)
    w2 = jnp.swapaxes(w_conv2, 3, 4)

    halo = lax.ppermute(volumes[:, :, 3], SLABS, forward)
    held_own, held_slope, away = call(
        first_kernel,
        [((sum(OWN), WIDE), BF), ((128, WIDE), BF), ((64, WIDE), BF)],
        (volumes, w1, w2, split, own),
        flops=10**9,
    )
    got = lax.ppermute(away, SLABS, forward)
    held_near, part, part_back = call(
        second_kernel,
        [((sum(NEAR), WIDE), BF), ((64, WIDE), F32), ((64, WIDE), BF)],
        (halo, split, w1, own, rim, w2, held_own, held_slope),
        flops=2 * 10**9,
    )
    part_next = lax.ppermute(part_back, SLABS, backward)
    slope2, pay, fown = call(
        third_kernel,
        [((64, WIDE), BF), ((32, 8, LANES), BF), ((S, LANES), BF)],
        (part, got),
        flops=3 * 10**9,
    )
    gathered = lax.all_to_all(pay, SLABS, 0, 0, tiled=True)
    next2, wd1, block = call(
        between_kernel,
        [((64, WIDE), BF), ((2048, LANES), BF), ((256, 256), BF)],
        (part_next, away, w_dense1, w2),
        scratch=[pltpu.VMEM((2048, LANES), F32)],
        flops=10**8,
    )
    gf, mix, small = call(
        tail_kernel,
        [((LANES, S), F32), ((LANES, LANES), F32), ((8, LANES), F32)],
        (gathered, wd1, w_dense2.T, w_dense3.T, targets.T, fown),
        scalars=(counts, position),
        scratch=[pltpu.VMEM((LANES, LANES), F32)],
        flops=2000000000,
    )
    (scattered,) = call(
        back_kernel,
        [((16, 48, LANES), BF)],
        (gf, mix, small, held_own, block, slope2, next2, held_near),
        scratch=[
            pltpu.VMEM((256, WIDE), BF), pltpu.VMEM((2, 128, WIDE), BF),
            pltpu.VMEM((16 * PART, LANES), F32), pltpu.VMEM((192, LANES), F32),
            pltpu.VMEM((48, LANES), F32),
        ],
        flops=2 * 10**9,
    )
    over_group = lax.all_to_all(scattered, (*DP, "core"), 0, 0, tiled=True)
    to_column, d2, d3, loss = call(
        group_kernel,
        [((16, 32, LANES), BF), ((8, LANES), F32), ((4, 64), F32), ((1, 1), F32)],
        (over_group,),
    )
    over_column = lax.all_to_all(to_column, COLUMN, 0, 0, tiled=True)
    (back,) = call(
        column_kernel, [((8, 160, LANES), BF)], (over_column, d2)
    )
    summed = lax.all_to_all(back, DP, 0, 0, tiled=True)
    other = lax.ppermute(summed, "core", swap)
    gw1, gw2, gd1, gd2 = call(
        last_kernel,
        [
            ((3, 3, 3, 4, 32), F32), ((3, 3, 3, 32, 64), F32),
            ((2048, LANES), F32), ((64, LANES), F32),
        ],
        (summed, other),
        scalars=(core,),
        scratch=[pltpu.VMEM((16 * PART, LANES), F32), pltpu.VMEM((16, LANES, LANES), F32)],
    )
    return (
        loss.reshape(()), jnp.swapaxes(gw1, 3, 4), jnp.swapaxes(gw2, 3, 4), gd1, gd2.T, d3.T,
    )


def solution(mesh):
    fine = Mesh(mesh.devices.reshape(4, 2, 2, 8, 2), ("x", "yl", "yh", "z", "core"))
    placed = (P(DP, None, SLABS, None, None), P(DP, None), P(), P(), P(), P(), P(), P())
    return jax.shard_map(
        local, mesh=fine, in_specs=placed, out_specs=(P(), P(), P(), P(), P(), P()), check_vma=False
    )
```

```python
import functools

import jax
import jax.numpy as jnp
import numpy as np
from jax import lax
from jax.experimental import pallas as pl
from jax.experimental.pallas import tpu as pltpu
from jax.sharding import Mesh
from jax.sharding import PartitionSpec as P

BF = jnp.bfloat16
F32 = jnp.float32
SLABS = ("yh", "z", "core")
DP = ("x", "yl")
COLUMN = ("yh", "z")
S = 16
LANES = 128
WIDE = S * LANES
CHUNK = 2048
MANY = WIDE // CHUNK
PER = CHUNK // LANES
PART = 24
SMALL = 16 * 1024 * 1024

NN = (((1,), (0,)), ((), ()))
NT = (((1,), (1,)), ((), ()))
TN = (((0,), (0,)), ((), ()))


def mm(a, b, dims=NN):
    return lax.dot_general(a, b, dims, preferred_element_type=F32)


def three(x):
    high = x.astype(BF)
    rest = x - high.astype(F32)
    mid = rest.astype(BF)
    return high, mid, (rest - mid.astype(F32)).astype(BF)


def leaky(v, t):
    return v * (0.65 + 0.35 * t)


def slope(v, t):
    return 0.65 + 0.35 * t + 0.35 * v * (1.0 - t * t)


def lane_ids(shape):
    return lax.broadcasted_iota(jnp.int32, shape, len(shape) - 1)


def shift_up(x):
    parts = []
    for k in range(x.shape[1] // LANES):
        p = pltpu.roll(x[:, k * LANES : (k + 1) * LANES], 1, 1)
        parts.append(jnp.where(lane_ids(p.shape) == 0, 0.0, p))
    return jnp.concatenate(parts, axis=1)


def shift_down(x):
    parts = []
    for k in range(x.shape[1] // LANES):
        p = pltpu.roll(x[:, k * LANES : (k + 1) * LANES], LANES - 1, 1)
        parts.append(jnp.where(lane_ids(p.shape) == LANES - 1, 0.0, p))
    return jnp.concatenate(parts, axis=1)


def call(kernel, outs, args, scalars=(), scratch=(), vmem=SMALL, flops=10**8):
    size = sum(int(np.prod(s)) * jnp.dtype(d).itemsize for s, d in outs)
    return pl.pallas_call(
        kernel,
        out_shape=[jax.ShapeDtypeStruct(s, d) for s, d in outs],
        in_specs=[pl.BlockSpec(memory_space=pltpu.SMEM)] * len(scalars)
        + [pl.BlockSpec(memory_space=pltpu.VMEM)] * len(args),
        out_specs=[pl.BlockSpec(memory_space=pltpu.VMEM)] * len(outs),
        scratch_shapes=list(scratch),
        compiler_params=pltpu.CompilerParams(vmem_limit_bytes=vmem),
        cost_estimate=pl.CostEstimate(flops=flops, bytes_accessed=size, transcendentals=0),
    )(*scalars, *args)


def parts(ref, *heights):
    out, at = [], 0
    for h in heights:
        out.append(ref.at[at : at + h])
        at += h
    return out


def bands(taps, ref, *index):
    return jnp.concatenate([mm(taps, ref[(*index, j)], TN).astype(BF) for j in range(2)], axis=0)


def band_here(i, j, planes):
    row = lax.broadcasted_iota(jnp.int32, (108, 1), 0)
    tap = lax.shift_right_logical(row, 2)
    third = lax.shift_right_logical(tap * 43, 7)
    a = lax.shift_right_logical(third * 43, 7)
    e, b = tap - 3 * third, third - 3 * a
    row_key = (e * 4 + jnp.bitwise_and(row, 3)) * 64 + a * 8 + b
    col = lax.broadcasted_iota(jnp.int32, (1, 48 * planes), 1)
    y = jnp.bitwise_and(col, 3) - 2 * j + 1
    if planes == 4:
        x = jnp.bitwise_and(lax.shift_right_logical(col, 2), 3) - 2 * i + 1
        col_key = lax.shift_right_logical(col, 4) * 64 + x * 8 + y
    else:
        col_key = lax.shift_right_logical(col, 2) * 64 + y
    return jnp.where(row_key == col_key, 1.0, 0.0).astype(BF)


def store_plane(h, s, cols, a1_ref, slope_ref):
    t = jnp.tanh(h)
    act = leaky(h, t)
    slope_ref[s * 64 : (s + 1) * 64, cols] = slope(h, t).astype(BF)
    if s == 0:
        a1_ref[64:128, cols] = act.astype(BF)
    else:
        a1_ref[128:192, cols] = act.astype(BF)
        a1_ref[0:64, cols] = shift_up(act).astype(BF)


def taps_of(w2_ref, a):
    return jnp.concatenate([w2_ref[a, b, e] for e in range(3) for b in (1, 2)], axis=0)


def bands(taps, ref, *index):
    return jnp.concatenate([mm(taps, ref[(*index, j)], TN).astype(BF) for j in range(2)], axis=0)


OWN = (320, 192)
NEAR = (80, 192, 128, 128)


def separate(rows, split, out_ref, height, first, many):
    d = mm(rows, split[...])
    for k in range(5):
        for n in range(many):
            at = (first + n) * LANES
            out_ref[k * height : (k + 1) * height, at : at + LANES] = d[
                n * height : (n + 1) * height, k * LANES : (k + 1) * LANES
            ].astype(BF)


def matrices_kernel(split_ref, own_ref, rim_ref):
    z = lax.broadcasted_iota(jnp.int32, (512, LANES), 0)
    m = lax.broadcasted_iota(jnp.int32, (512, LANES), 1)
    for k in range(5):
        split_ref[:, k * LANES : (k + 1) * LANES] = jnp.where(z - 4 * m == k - 1, 1.0, 0.0).astype(BF)
    for j in range(2):
        for i in range(2):
            own_ref[i, j] = band_here(i, j, 4)
        rim_ref[j] = band_here(0, j, 1)


def first_kernel(v, w1, w2, split, own, out_ref, slope_ref, away_ref):
    x4_ref, a1_ref = parts(out_ref, *OWN)
    w = bands(w1[...].reshape(108, 32), own, 1)
    w2a = taps_of(w2, 0)
    for q in range(MANY):
        rows = jnp.concatenate([v[PER * q + n].reshape(64, 512) for n in range(PER)], axis=0)
        separate(rows, split, x4_ref, 64, PER * q, PER)
    for q in range(MANY):
        cols = slice(q * CHUNK, (q + 1) * CHUNK)
        for s in range(2):
            h = mm(w, x4_ref[s * 128 : s * 128 + 192, cols])
            store_plane(h, s, cols, a1_ref, slope_ref)
    for q in range(MANY):
        cols = slice(q * CHUNK, (q + 1) * CHUNK)
        away_ref[:, cols] = mm(w2a, a1_ref[:, cols], TN).astype(BF)


def second_kernel(
    halo, split, w1, own, rim, w2, first_ref, s1c, out_ref, part_ref, back_ref
):
    x4, a1c = parts(first_ref, *OWN)
    xh_ref, a1_ref, slope_ref, slope_c_ref = parts(out_ref, *NEAR)
    slope_c_ref[...] = s1c[...]
    taps = w1[...].reshape(108, 32)
    w, wh = bands(taps, own, 0), bands(taps, rim)
    rows = jnp.concatenate([halo[n].reshape(16, 512) for n in range(S)], axis=0)
    separate(rows, split, xh_ref, 16, 0, S)
    taps_b, taps_c = taps_of(w2, 1), taps_of(w2, 2)
    for q in range(MANY):
        cols = slice(q * CHUNK, (q + 1) * CHUNK)
        for s in range(2):
            h = mm(w, x4[s * 128 : s * 128 + 192, cols]) + mm(
                wh, xh_ref[s * 32 : s * 32 + 48, cols]
            )
            store_plane(h, s, cols, a1_ref, slope_ref)
    for q in range(MANY):
        cols = slice(q * CHUNK, (q + 1) * CHUNK)
        part = mm(taps_b, a1_ref[:, cols], TN) + mm(taps_c, a1c[:, cols], TN)
        part_ref[:, cols] = part
        back_ref[:, cols] = part.astype(BF)


def between_kernel(part, away, wd1, w2, next2_ref, wd1_ref, block_ref, wide_ref):
    for q in range(MANY):
        cols = slice(q * CHUNK, (q + 1) * CHUNK)
        h2 = part[:, cols].astype(F32) + away[:, cols].astype(F32)
        next2_ref[:, cols] = slope(h2, jnp.tanh(h2)).astype(BF)

    def tap(a, e):
        return jnp.concatenate([w2[a, 1, e], w2[a, 2, e]], axis=0)

    zero = jnp.zeros((64, 64), BF)
    for k, row in enumerate(
        (
            (tap(1, 1), zero, zero, zero),
            (tap(2, 1), tap(0, 1), zero, zero),
            (tap(1, 2), zero, tap(1, 0), zero),
            (tap(2, 2), tap(0, 2), tap(2, 0), tap(0, 0)),
        )
    ):
        block_ref[k * 64 : (k + 1) * 64] = jnp.concatenate(row, axis=1)
    wide_ref[...] = wd1[...].astype(F32)
    for x in range(32):
        wd1_ref[x * 64 : (x + 1) * 64] = wide_ref[pl.ds(x, 64, stride=32), :].astype(BF)


def third_kernel(part, got, slope2_ref, pay_ref, fown_ref):
    total = jnp.zeros((S, 64), F32)
    for q in range(MANY):
        cols = slice(q * CHUNK, (q + 1) * CHUNK)
        h2 = part[:, cols] + got[:, cols].astype(F32)
        t = jnp.tanh(h2)
        act2 = leaky(h2, t).astype(BF)
        slope2_ref[:, cols] = slope(h2, t).astype(BF)
        rows = lax.broadcasted_iota(jnp.int32, (S, CHUNK), 0)
        owner = lax.shift_right_logical(lane_ids((S, CHUNK)), 7) + PER * q
        pick = jnp.where(rows == owner, 1.0, 0.0).astype(BF)
        total = total + mm(pick, act2, NT)
    feats = total * (1.0 / 128.0)
    pay = jnp.concatenate([feats[0:8], feats[8:16]], axis=1).astype(BF)
    for x in range(32):
        pay_ref[x] = pay
    fown_ref[...] = jnp.concatenate([feats, jnp.zeros((S, 64), F32)], axis=1).astype(BF)


def tail_kernel(
    counts, position, g, wd1, wd2, wd3, targets, fown, gf_ref, mix_ref, small_ref, padded_ref
):
    ends = []
    for k in range(32):
        ends.append(counts[k] + (ends[-1] if k else 0))
    by_row = lax.broadcasted_iota(jnp.int32, (S, S), 0)
    by_col = lax.broadcasted_iota(jnp.int32, (S, S), 1)
    row_owner = jnp.zeros((S, S), jnp.int32)
    col_owner = jnp.zeros((S, S), jnp.int32)
    for end in ends:
        row_owner = row_owner + jnp.where(by_row >= end, 1, 0)
        col_owner = col_owner + jnp.where(by_col >= end, 1, 0)
    alike = jnp.where(row_owner == col_owner, 1.0, 0.0)
    same = (alike / jnp.sum(alike, axis=1, keepdims=True)).astype(BF)
    same = jnp.concatenate([same] * 3, axis=1)

    low = lane_ids((8, LANES)) < 64
    pairs = []
    for p in range(16):
        ga, gb = g[2 * p].astype(F32), g[2 * p + 1].astype(F32)
        lo = jnp.where(low, ga, pltpu.roll(gb, 64, 1))
        hi = jnp.where(low, pltpu.roll(ga, 64, 1), gb)
        pairs.append(jnp.concatenate([lo, hi], axis=0).astype(BF))
    feats = jnp.concatenate(pairs, axis=1)
    dense1 = mm(feats, wd1[...])
    centred = dense1 - 0.5 * mm(same, jnp.concatenate(three(dense1), axis=0))
    t1 = jnp.tanh(centred)
    out1 = leaky(centred, t1).astype(BF)

    w2 = jnp.concatenate([wd2[...], jnp.zeros((64, LANES), BF)], axis=0)
    padded_ref[...] = jnp.zeros((LANES, LANES), F32)
    padded_ref[64:68, 0:64] = wd3[...].astype(F32)
    w3 = padded_ref[...].astype(BF)
    padded_ref[...] = jnp.zeros((LANES, LANES), F32)
    padded_ref[64:68, 0:S] = targets[...]
    goal = jnp.transpose(padded_ref[...], (1, 0))[0:S]

    dense2 = mm(out1, w2, NT)
    t2 = jnp.tanh(dense2)
    out2 = leaky(dense2, t2).astype(BF)
    diff = mm(out2, w3, NT) - goal
    loss = jnp.sum(jnp.sum(diff * diff, axis=1, keepdims=True), axis=0, keepdims=True) / 32.0
    gpred = (diff / 16.0).astype(BF)
    gdense2 = (mm(gpred, w3) * slope(dense2, t2)).astype(BF)
    gcentred = mm(gdense2, w2) * slope(centred, t1)
    gdense1 = (gcentred - 0.5 * mm(same, jnp.concatenate(three(gcentred), axis=0))).astype(BF)
    here = position[0]
    after = jnp.minimum(here + 1, 31)
    for k, slab in enumerate((here, after)):
        rows = wd1[pl.ds(pl.multiple_of(slab * 64, 64), 64), :]
        gf_ref[k * 64 : (k + 1) * 64] = mm(rows, gdense1, NT)
    gf_ref[64:128] = jnp.where(here < 31, gf_ref[64:128], 0.0)

    d1 = mm(fown[...], gdense1, TN)
    d2 = mm(gdense2, out1, TN)
    d3 = mm(gpred, out2, TN)[64:72]
    lanes = lane_ids((8, LANES))
    top = lax.broadcasted_iota(jnp.int32, (8, LANES), 0) == 0
    for k, piece in enumerate(three(loss)):
        d3 = jnp.where(jnp.logical_and(top, lanes == 64 + k), piece.astype(F32), d3)
    small_ref[...] = d3
    for k in range(8):
        pair = d1[k * 8 : (k + 1) * 8], d2[k * 8 : (k + 1) * 8]
        mix_ref[k * 16 : k * 16 + 8] = low_half(*pair)
        mix_ref[k * 16 + 8 : k * 16 + 16] = high_half(*pair)


def tap_sums(r_ref, rh_ref):
    group = lax.shift_right_logical(lane_ids((12, LANES)), 5)
    sums = [jnp.zeros((12, LANES), F32) for _ in range(9)]

    def add(rows, places):
        for g, a, b in places:
            if 0 <= a < 3 and 0 <= b < 3:
                sums[a * 3 + b] = sums[a * 3 + b] + jnp.where(group == g, rows, 0.0)

    for y in range(4):
        for x in range(4):
            add(
                r_ref[pl.ds(x * 4 + y, 12, stride=16), :],
                [(2 * i + j, x - 2 * i + 1, y - 2 * j + 1) for i in range(2) for j in range(2)],
            )
        add(rh_ref[pl.ds(y, 12, stride=4), :], [(j, 0, y - 2 * j + 1) for j in range(2)])
    out = []
    for total in sums:
        total = total + pltpu.roll(total, 64, 1)
        out.append(total + pltpu.roll(total, 32, 1))
    return out


def back_kernel(
    gf_ref, mix, small, first_ref, block, slope2, next2, near, out_ref,
    g_ref, h_ref, w_ref, r_ref, rh_ref,
):
    x4, a1c = parts(first_ref, *OWN)
    gf = gf_ref[...].astype(BF).astype(F32) * (1.0 / 128.0)
    for q in range(MANY):
        cols = slice(q * CHUNK, (q + 1) * CHUNK)
        spread = jnp.concatenate(
            [jnp.broadcast_to(gf[:, PER * q + n : PER * q + n + 1], (128, LANES)) for n in range(PER)],
            axis=1,
        )
        go = spread[0:64] * slope2[:, cols].astype(F32)
        gn = spread[64:128] * next2[:, cols].astype(F32)
        g_ref[0:64, cols] = go.astype(BF)
        g_ref[64:128, cols] = gn.astype(BF)
        g_ref[128:192, cols] = shift_down(go).astype(BF)
        g_ref[192:256, cols] = shift_down(gn).astype(BF)
        gact = mm(block[...], g_ref[:, cols])
        s1b, s1c = parts(near, *NEAR)[2:]
        for s in range(2):
            for i, s1 in enumerate((s1b, s1c)):
                r = (2 * s + i) * 64
                h_ref[s, i * 64 : (i + 1) * 64, cols] = (
                    gact[r : r + 64] * s1[s * 64 : (s + 1) * 64, cols].astype(F32)
                ).astype(BF)
    xh, a1b = parts(near, *NEAR)[:2]
    both = mm(jnp.concatenate([a1c[...], a1b[...]], axis=0), g_ref[0:128, :], NT)
    w_ref[0:192] = both[0:192]
    w_ref[192:288] = jnp.concatenate([both[192:288, 0:64], both[288:384, 0:64]], axis=1)
    bands_of = [
        mm(
            jnp.concatenate([x4[128 * s : 128 * s + 192, :], xh[32 * s : 32 * s + 48, :]], axis=0),
            h_ref[s],
            NT,
        )
        for s in range(2)
    ]
    r_ref[...] = bands_of[0][0:192] + bands_of[1][0:192]
    rh_ref[...] = bands_of[0][192:240] + bands_of[1][192:240]
    sums = tap_sums(r_ref, rh_ref)
    group = lax.shift_right_logical(lane_ids((12, LANES)), 5)
    w_ref[288:384] = jnp.zeros((96, LANES), F32)
    for k in range(3):
        packed = sums[4 * k]
        for n in range(1, 4):
            if 4 * k + n < 9:
                packed = jnp.where(group == n, sums[4 * k + n], packed)
        w_ref[288 + 16 * k : 300 + 16 * k] = packed
    zero = jnp.zeros((8, LANES), F32)
    for p in range(16):
        out_ref[p] = jnp.concatenate(
            [w_ref[p * PART : (p + 1) * PART], small[...], mix[p * 8 : (p + 1) * 8], zero], axis=0
        ).astype(BF)


def low_half(a, b):
    rows = lax.broadcasted_iota(jnp.int32, (8, LANES), 0)
    return jnp.where(rows < 4, a, pltpu.roll(b, 4, 0))


def high_half(a, b):
    rows = lax.broadcasted_iota(jnp.int32, (8, LANES), 0)
    return jnp.where(rows < 4, pltpu.roll(a, 4, 0), b)


def group_kernel(got, out_ref, d2_ref, d3_ref, loss_ref):
    even, odd = got[0].astype(F32), got[1].astype(F32)
    for k in range(1, 8):
        even, odd = even + got[2 * k].astype(F32), odd + got[2 * k + 1].astype(F32)
    total = even[0:PART] + odd[0:PART]
    d1 = low_half(even[32:40], odd[32:40])
    pay = jnp.concatenate([total, d1], axis=0).astype(BF)
    for k in range(16):
        out_ref[k] = pay
    d2_ref[...] = pltpu.roll(even[32:40], 4, 0)
    small = even[PART:32]
    d3_ref[...] = small[0:4, 0:64]
    lanes = lane_ids((8, LANES))
    rows = lax.broadcasted_iota(jnp.int32, (8, LANES), 0)
    held = jnp.logical_and(jnp.logical_and(lanes >= 64, lanes < 67), rows == 0)
    values = jnp.where(held, small, 0.0)
    loss_ref[...] = jnp.sum(jnp.sum(values, axis=1, keepdims=True), axis=0, keepdims=True)


def column_kernel(got, d2, out_ref):
    blocks = [got[k].astype(F32) for k in range(16)]
    total = blocks[0][0:PART]
    for b in blocks[1:]:
        total = total + b[0:PART]
    pay = jnp.concatenate([total, d2[...]] + [b[PART:32] for b in blocks], axis=0).astype(BF)
    for k in range(8):
        out_ref[k] = pay


def last_kernel(core, mine, other, gw1_ref, gw2_ref, gd1_ref, gd2_ref, w_ref, t_ref):
    first = core[0] == 0
    for k in range(8):
        for n, chunk in enumerate((mine, other)):
            t_ref[2 * k + n] = chunk[k, 32:160].astype(F32)
            base = k * 256 + jnp.bitwise_xor(core[0], n) * 128
            for r in range(4):
                at = pl.multiple_of(base + r * 32, 32)
                gd1_ref[pl.ds(at, 32), :] = t_ref[2 * k + n, pl.ds(r, 32, stride=4), :]
        a, b = mine[k, 0:32].astype(F32), other[k, 0:32].astype(F32)
        low, high = jnp.where(first, a, b), jnp.where(first, b, a)
        w_ref[2 * k * PART : (2 * k + 1) * PART] = low[0:PART]
        w_ref[(2 * k + 1) * PART : (2 * k + 2) * PART] = high[0:PART]
        gd2_ref[k * 8 : (k + 1) * 8] = low_half(low[PART:32], high[PART:32])
    for a in range(3):
        for e in range(3):
            gw2_ref[a, 0, e] = jnp.zeros((32, 64), F32)
            for b in (1, 2):
                at = e * 64 + (b - 1) * 32
                right = a == 0
                if a == 1:
                    right = at >= 96
                    at = 192 + at % 96
                block = w_ref[at : at + 32]
                if right:
                    block = pltpu.roll(block, 64, 1)
                gw2_ref[a, b, e] = block[:, 0:64]
    for a in range(3):
        for b in range(3):
            k, n = divmod(a * 3 + b, 4)
            packed = w_ref[288 + 16 * k : 304 + 16 * k]
            if n:
                packed = pltpu.roll(packed, LANES - 32 * n, 1)
            for e in range(3):
                gw1_ref[a, b, e] = packed[4 * e : 4 * e + 4, 0:32]


def local(volumes, targets, counts, w_conv1, w_conv2, w_dense1, w_dense2, w_dense3):
    core = lax.axis_index("core").astype(jnp.int32).reshape(1)
    position = lax.axis_index(SLABS).astype(jnp.int32).reshape(1)
    forward = [(i, i + 1) for i in range(31)]
    backward = [(i + 1, i) for i in range(31)]
    swap = [(0, 1), (1, 0)]
    split, own, rim = call(
        matrices_kernel,
        [((512, 640), BF), ((2, 2, 108, 192), BF), ((2, 108, 48), BF)],
        (),
        flops=2 * 10**9,
    )
    w1 = jnp.swapaxes(w_conv1, 3, 4).reshape(27, 4, 32)
    w2 = jnp.swapaxes(w_conv2, 3, 4)

    halo = lax.ppermute(volumes[:, :, 3], SLABS, forward)
    held_own, held_slope, away = call(
        first_kernel,
        [((sum(OWN), WIDE), BF), ((128, WIDE), BF), ((64, WIDE), BF)],
        (volumes, w1, w2, split, own),
        flops=10**9,
    )
    got = lax.ppermute(away, SLABS, forward)
    held_near, part, part_back = call(
        second_kernel,
        [((sum(NEAR), WIDE), BF), ((64, WIDE), F32), ((64, WIDE), BF)],
        (halo, split, w1, own, rim, w2, held_own, held_slope),
        flops=2 * 10**9,
    )
    part_next = lax.ppermute(part_back, SLABS, backward)
    slope2, pay, fown = call(
        third_kernel,
        [((64, WIDE), BF), ((32, 8, LANES), BF), ((S, LANES), BF)],
        (part, got),
        flops=3 * 10**9,
    )
    gathered = lax.all_to_all(pay, SLABS, 0, 0, tiled=True)
    next2, wd1, block = call(
        between_kernel,
        [((64, WIDE), BF), ((2048, LANES), BF), ((256, 256), BF)],
        (part_next, away, w_dense1, w2),
        scratch=[pltpu.VMEM((2048, LANES), F32)],
        flops=10**8,
    )
    gf, mix, small = call(
        tail_kernel,
        [((LANES, S), F32), ((LANES, LANES), F32), ((8, LANES), F32)],
        (gathered, wd1, w_dense2.T, w_dense3.T, targets.T, fown),
        scalars=(counts, position),
        scratch=[pltpu.VMEM((LANES, LANES), F32)],
        flops=2000000000,
    )
    (scattered,) = call(
        back_kernel,
        [((16, 48, LANES), BF)],
        (gf, mix, small, held_own, block, slope2, next2, held_near),
        scratch=[
            pltpu.VMEM((256, WIDE), BF), pltpu.VMEM((2, 128, WIDE), BF),
            pltpu.VMEM((16 * PART, LANES), F32), pltpu.VMEM((192, LANES), F32),
            pltpu.VMEM((48, LANES), F32),
        ],
        flops=2 * 10**9,
    )
    over_group = lax.all_to_all(scattered, (*DP, "core"), 0, 0, tiled=True)
    to_column, d2, d3, loss = call(
        group_kernel,
        [((16, 32, LANES), BF), ((8, LANES), F32), ((4, 64), F32), ((1, 1), F32)],
        (over_group,),
    )
    over_column = lax.all_to_all(to_column, COLUMN, 0, 0, tiled=True)
    (back,) = call(
        column_kernel, [((8, 160, LANES), BF)], (over_column, d2)
    )
    summed = lax.all_to_all(back, DP, 0, 0, tiled=True)
    other = lax.ppermute(summed, "core", swap)
    gw1, gw2, gd1, gd2 = call(
        last_kernel,
        [
            ((3, 3, 3, 4, 32), F32), ((3, 3, 3, 32, 64), F32),
            ((2048, LANES), F32), ((64, LANES), F32),
        ],
        (summed, other),
        scalars=(core,),
        scratch=[pltpu.VMEM((16 * PART, LANES), F32), pltpu.VMEM((16, LANES, LANES), F32)],
    )
    return (
        loss.reshape(()), jnp.swapaxes(gw1, 3, 4), jnp.swapaxes(gw2, 3, 4), gd1, gd2.T, d3.T,
    )


def solution(mesh):
    fine = Mesh(mesh.devices.reshape(4, 2, 2, 8, 2), ("x", "yl", "yh", "z", "core"))
    placed = (P(DP, None, SLABS, None, None), P(DP, None), P(), P(), P(), P(), P(), P())
    return jax.shard_map(
        local, mesh=fine, in_specs=placed, out_specs=(P(), P(), P(), P(), P(), P()), check_vma=False
    )
```

```python
import functools

import jax
import jax.numpy as jnp
import numpy as np
from jax import lax
from jax.experimental import pallas as pl
from jax.experimental.pallas import tpu as pltpu
from jax.sharding import Mesh
from jax.sharding import PartitionSpec as P

BF = jnp.bfloat16
F32 = jnp.float32
SLABS = ("yh", "z", "core")
DP = ("x", "yl")
COLUMN = ("yh", "z")
S = 16
LANES = 128
WIDE = S * LANES
CHUNK = 2048
MANY = WIDE // CHUNK
PER = CHUNK // LANES
PART = 24
SMALL = 16 * 1024 * 1024

NN = (((1,), (0,)), ((), ()))
NT = (((1,), (1,)), ((), ()))
TN = (((0,), (0,)), ((), ()))


def mm(a, b, dims=NN):
    return lax.dot_general(a, b, dims, preferred_element_type=F32)


def three(x):
    high = x.astype(BF)
    rest = x - high.astype(F32)
    mid = rest.astype(BF)
    return high, mid, (rest - mid.astype(F32)).astype(BF)


def leaky(v, t):
    return v * (0.65 + 0.35 * t)


def slope(v, t):
    return 0.65 + 0.35 * t + 0.35 * v * (1.0 - t * t)


def lane_ids(shape):
    return lax.broadcasted_iota(jnp.int32, shape, len(shape) - 1)


def shift_up(x):
    parts = []
    for k in range(x.shape[1] // LANES):
        p = pltpu.roll(x[:, k * LANES : (k + 1) * LANES], 1, 1)
        parts.append(jnp.where(lane_ids(p.shape) == 0, 0.0, p))
    return jnp.concatenate(parts, axis=1)


def shift_down(x):
    parts = []
    for k in range(x.shape[1] // LANES):
        p = pltpu.roll(x[:, k * LANES : (k + 1) * LANES], LANES - 1, 1)
        parts.append(jnp.where(lane_ids(p.shape) == LANES - 1, 0.0, p))
    return jnp.concatenate(parts, axis=1)


def call(kernel, outs, args, scalars=(), scratch=(), vmem=SMALL, flops=10**8):
    size = sum(int(np.prod(s)) * jnp.dtype(d).itemsize for s, d in outs)
    return pl.pallas_call(
        kernel,
        out_shape=[jax.ShapeDtypeStruct(s, d) for s, d in outs],
        in_specs=[pl.BlockSpec(memory_space=pltpu.SMEM)] * len(scalars)
        + [pl.BlockSpec(memory_space=pltpu.VMEM)] * len(args),
        out_specs=[pl.BlockSpec(memory_space=pltpu.VMEM)] * len(outs),
        scratch_shapes=list(scratch),
        compiler_params=pltpu.CompilerParams(vmem_limit_bytes=vmem),
        cost_estimate=pl.CostEstimate(flops=flops, bytes_accessed=size, transcendentals=0),
    )(*scalars, *args)


def parts(ref, *heights):
    out, at = [], 0
    for h in heights:
        out.append(ref.at[at : at + h])
        at += h
    return out


def bands(taps, ref, *index):
    return jnp.concatenate([mm(taps, ref[(*index, j)], TN).astype(BF) for j in range(2)], axis=0)


def band_here(i, j, planes):
    row = lax.broadcasted_iota(jnp.int32, (108, 1), 0)
    tap = lax.shift_right_logical(row, 2)
    third = lax.shift_right_logical(tap * 43, 7)
    a = lax.shift_right_logical(third * 43, 7)
    e, b = tap - 3 * third, third - 3 * a
    row_key = (e * 4 + jnp.bitwise_and(row, 3)) * 64 + a * 8 + b
    col = lax.broadcasted_iota(jnp.int32, (1, 48 * planes), 1)
    y = jnp.bitwise_and(col, 3) - 2 * j + 1
    if planes == 4:
        x = jnp.bitwise_and(lax.shift_right_logical(col, 2), 3) - 2 * i + 1
        col_key = lax.shift_right_logical(col, 4) * 64 + x * 8 + y
    else:
        col_key = lax.shift_right_logical(col, 2) * 64 + y
    return jnp.where(row_key == col_key, 1.0, 0.0).astype(BF)


def store_plane(h, s, cols, a1_ref, slope_ref):
    t = jnp.tanh(h)
    act = leaky(h, t)
    slope_ref[s * 64 : (s + 1) * 64, cols] = slope(h, t).astype(BF)
    if s == 0:
        a1_ref[64:128, cols] = act.astype(BF)
    else:
        a1_ref[128:192, cols] = act.astype(BF)
        a1_ref[0:64, cols] = shift_up(act).astype(BF)


def taps_of(w2_ref, a):
    return jnp.concatenate([w2_ref[a, b, e] for e in range(3) for b in (1, 2)], axis=0)


def bands(taps, ref, *index):
    return jnp.concatenate([mm(taps, ref[(*index, j)], TN).astype(BF) for j in range(2)], axis=0)


OWN = (320, 192)
NEAR = (80, 192, 128, 128)


def separate(rows, split, out_ref, height, first, many):
    d = mm(rows, split[...])
    for k in range(5):
        for n in range(many):
            at = (first + n) * LANES
            out_ref[k * height : (k + 1) * height, at : at + LANES] = d[
                n * height : (n + 1) * height, k * LANES : (k + 1) * LANES
            ].astype(BF)


def matrices_kernel(split_ref, own_ref, rim_ref):
    z = lax.broadcasted_iota(jnp.int32, (512, LANES), 0)
    m = lax.broadcasted_iota(jnp.int32, (512, LANES), 1)
    for k in range(5):
        split_ref[:, k * LANES : (k + 1) * LANES] = jnp.where(z - 4 * m == k - 1, 1.0, 0.0).astype(BF)
    for j in range(2):
        for i in range(2):
            own_ref[i, j] = band_here(i, j, 4)
        rim_ref[j] = band_here(0, j, 1)


def first_kernel(v, w1, w2, split, own, out_ref, slope_ref, away_ref):
    x4_ref, a1_ref = parts(out_ref, *OWN)
    w = bands(w1[...].reshape(108, 32), own, 1)
    w2a = taps_of(w2, 0)
    for q in range(MANY):
        rows = jnp.concatenate([v[PER * q + n].reshape(64, 512) for n in range(PER)], axis=0)
        separate(rows, split, x4_ref, 64, PER * q, PER)
    for q in range(MANY):
        cols = slice(q * CHUNK, (q + 1) * CHUNK)
        for s in range(2):
            h = mm(w, x4_ref[s * 128 : s * 128 + 192, cols])
            store_plane(h, s, cols, a1_ref, slope_ref)
    for q in range(MANY):
        cols = slice(q * CHUNK, (q + 1) * CHUNK)
        away_ref[:, cols] = mm(w2a, a1_ref[:, cols], TN).astype(BF)


def second_kernel(
    halo, split, w1, own, rim, w2, first_ref, s1c, out_ref, part_ref, back_ref
):
    x4, a1c = parts(first_ref, *OWN)
    xh_ref, a1_ref, slope_ref, slope_c_ref = parts(out_ref, *NEAR)
    slope_c_ref[...] = s1c[...]
    taps = w1[...].reshape(108, 32)
    w, wh = bands(taps, own, 0), bands(taps, rim)
    rows = jnp.concatenate([halo[n].reshape(16, 512) for n in range(S)], axis=0)
    separate(rows, split, xh_ref, 16, 0, S)
    taps_b, taps_c = taps_of(w2, 1), taps_of(w2, 2)
    for q in range(MANY):
        cols = slice(q * CHUNK, (q + 1) * CHUNK)
        for s in range(2):
            h = mm(w, x4[s * 128 : s * 128 + 192, cols]) + mm(
                wh, xh_ref[s * 32 : s * 32 + 48, cols]
            )
            store_plane(h, s, cols, a1_ref, slope_ref)
    for q in range(MANY):
        cols = slice(q * CHUNK, (q + 1) * CHUNK)
        part = mm(taps_b, a1_ref[:, cols], TN) + mm(taps_c, a1c[:, cols], TN)
        part_ref[:, cols] = part
        back_ref[:, cols] = part.astype(BF)


def between_kernel(part, away, wd1, w2, next2_ref, wd1_ref, block_ref, wide_ref):
    for q in range(MANY):
        cols = slice(q * CHUNK, (q + 1) * CHUNK)
        h2 = part[:, cols].astype(F32) + away[:, cols].astype(F32)
        next2_ref[:, cols] = slope(h2, jnp.tanh(h2)).astype(BF)

    def tap(a, e):
        return jnp.concatenate([w2[a, 1, e], w2[a, 2, e]], axis=0)

    zero = jnp.zeros((64, 64), BF)
    for k, row in enumerate(
        (
            (tap(1, 1), zero, zero, zero),
            (tap(2, 1), tap(0, 1), zero, zero),
            (tap(1, 2), zero, tap(1, 0), zero),
            (tap(2, 2), tap(0, 2), tap(2, 0), tap(0, 0)),
        )
    ):
        block_ref[k * 64 : (k + 1) * 64] = jnp.concatenate(row, axis=1)
    wide_ref[...] = wd1[...].astype(F32)
    for x in range(32):
        wd1_ref[x * 64 : (x + 1) * 64] = wide_ref[pl.ds(x, 64, stride=32), :].astype(BF)


def third_kernel(part, got, slope2_ref, pay_ref, fown_ref):
    total = jnp.zeros((S, 64), F32)
    for q in range(MANY):
        cols = slice(q * CHUNK, (q + 1) * CHUNK)
        h2 = part[:, cols] + got[:, cols].astype(F32)
        t = jnp.tanh(h2)
        act2 = leaky(h2, t).astype(BF)
        slope2_ref[:, cols] = slope(h2, t).astype(BF)
        rows = lax.broadcasted_iota(jnp.int32, (S, CHUNK), 0)
        owner = lax.shift_right_logical(lane_ids((S, CHUNK)), 7) + PER * q
        pick = jnp.where(rows == owner, 1.0, 0.0).astype(BF)
        total = total + mm(pick, act2, NT)
    feats = total * (1.0 / 128.0)
    pay = jnp.concatenate([feats[0:8], feats[8:16]], axis=1).astype(BF)
    for x in range(32):
        pay_ref[x] = pay
    fown_ref[...] = jnp.concatenate([feats, jnp.zeros((S, 64), F32)], axis=1).astype(BF)


def tail_kernel(
    counts, position, g, wd1, wd2, wd3, targets, fown, gf_ref, mix_ref, small_ref, padded_ref
):
    ends = []
    for k in range(32):
        ends.append(counts[k] + (ends[-1] if k else 0))
    by_row = lax.broadcasted_iota(jnp.int32, (S, S), 0)
    by_col = lax.broadcasted_iota(jnp.int32, (S, S), 1)
    row_owner = jnp.zeros((S, S), jnp.int32)
    col_owner = jnp.zeros((S, S), jnp.int32)
    for end in ends:
        row_owner = row_owner + jnp.where(by_row >= end, 1, 0)
        col_owner = col_owner + jnp.where(by_col >= end, 1, 0)
    alike = jnp.where(row_owner == col_owner, 1.0, 0.0)
    same = (alike / jnp.sum(alike, axis=1, keepdims=True)).astype(BF)
    same = jnp.concatenate([same] * 3, axis=1)

    low = lane_ids((8, LANES)) < 64
    pairs = []
    for p in range(16):
        ga, gb = g[2 * p].astype(F32), g[2 * p + 1].astype(F32)
        lo = jnp.where(low, ga, pltpu.roll(gb, 64, 1))
        hi = jnp.where(low, pltpu.roll(ga, 64, 1), gb)
        pairs.append(jnp.concatenate([lo, hi], axis=0).astype(BF))
    feats = jnp.concatenate(pairs, axis=1)
    dense1 = mm(feats, wd1[...])
    centred = dense1 - 0.5 * mm(same, jnp.concatenate(three(dense1), axis=0))
    t1 = jnp.tanh(centred)
    out1 = leaky(centred, t1).astype(BF)

    w2 = jnp.concatenate([wd2[...], jnp.zeros((64, LANES), BF)], axis=0)
    padded_ref[...] = jnp.zeros((LANES, LANES), F32)
    padded_ref[64:68, 0:64] = wd3[...].astype(F32)
    w3 = padded_ref[...].astype(BF)
    padded_ref[...] = jnp.zeros((LANES, LANES), F32)
    padded_ref[64:68, 0:S] = targets[...]
    goal = jnp.transpose(padded_ref[...], (1, 0))[0:S]

    dense2 = mm(out1, w2, NT)
    t2 = jnp.tanh(dense2)
    out2 = leaky(dense2, t2).astype(BF)
    diff = mm(out2, w3, NT) - goal
    loss = jnp.sum(jnp.sum(diff * diff, axis=1, keepdims=True), axis=0, keepdims=True) / 32.0
    gpred = (diff / 16.0).astype(BF)
    gdense2 = (mm(gpred, w3) * slope(dense2, t2)).astype(BF)
    gcentred = mm(gdense2, w2) * slope(centred, t1)
    gdense1 = (gcentred - 0.5 * mm(same, jnp.concatenate(three(gcentred), axis=0))).astype(BF)
    here = position[0]
    after = jnp.minimum(here + 1, 31)
    for k, slab in enumerate((here, after)):
        rows = wd1[pl.ds(pl.multiple_of(slab * 64, 64), 64), :]
        gf_ref[k * 64 : (k + 1) * 64] = mm(rows, gdense1, NT)
    gf_ref[64:128] = jnp.where(here < 31, gf_ref[64:128], 0.0)

    d1 = mm(fown[...], gdense1, TN)
    d2 = mm(gdense2, out1, TN)
    d3 = mm(gpred, out2, TN)[64:72]
    lanes = lane_ids((8, LANES))
    top = lax.broadcasted_iota(jnp.int32, (8, LANES), 0) == 0
    for k, piece in enumerate(three(loss)):
        d3 = jnp.where(jnp.logical_and(top, lanes == 64 + k), piece.astype(F32), d3)
    small_ref[...] = d3
    for k in range(8):
        pair = d1[k * 8 : (k + 1) * 8], d2[k * 8 : (k + 1) * 8]
        mix_ref[k * 16 : k * 16 + 8] = low_half(*pair)
        mix_ref[k * 16 + 8 : k * 16 + 16] = high_half(*pair)


def tap_sums(r_ref, rh_ref):
    group = lax.shift_right_logical(lane_ids((12, LANES)), 5)
    sums = [jnp.zeros((12, LANES), F32) for _ in range(9)]

    def add(rows, places):
        for g, a, b in places:
            if 0 <= a < 3 and 0 <= b < 3:
                sums[a * 3 + b] = sums[a * 3 + b] + jnp.where(group == g, rows, 0.0)

    for y in range(4):
        for x in range(4):
            add(
                r_ref[pl.ds(x * 4 + y, 12, stride=16), :],
                [(2 * i + j, x - 2 * i + 1, y - 2 * j + 1) for i in range(2) for j in range(2)],
            )
        add(rh_ref[pl.ds(y, 12, stride=4), :], [(j, 0, y - 2 * j + 1) for j in range(2)])
    out = []
    for total in sums:
        total = total + pltpu.roll(total, 64, 1)
        out.append(total + pltpu.roll(total, 32, 1))
    return out


def back_kernel(
    gf_ref, mix, small, first_ref, block, slope2, next2, near, out_ref,
    g_ref, h_ref, w_ref, r_ref, rh_ref,
):
    x4, a1c = parts(first_ref, *OWN)
    gf = gf_ref[...].astype(BF).astype(F32) * (1.0 / 128.0)
    for q in range(MANY):
        cols = slice(q * CHUNK, (q + 1) * CHUNK)
        spread = jnp.concatenate(
            [jnp.broadcast_to(gf[:, PER * q + n : PER * q + n + 1], (128, LANES)) for n in range(PER)],
            axis=1,
        )
        go = spread[0:64] * slope2[:, cols].astype(F32)
        gn = spread[64:128] * next2[:, cols].astype(F32)
        g_ref[0:64, cols] = go.astype(BF)
        g_ref[64:128, cols] = gn.astype(BF)
        g_ref[128:192, cols] = shift_down(go).astype(BF)
        g_ref[192:256, cols] = shift_down(gn).astype(BF)
        gact = mm(block[...], g_ref[:, cols])
        s1b, s1c = parts(near, *NEAR)[2:]
        for s in range(2):
            for i, s1 in enumerate((s1b, s1c)):
                r = (2 * s + i) * 64
                h_ref[s, i * 64 : (i + 1) * 64, cols] = (
                    gact[r : r + 64] * s1[s * 64 : (s + 1) * 64, cols].astype(F32)
                ).astype(BF)
    xh, a1b = parts(near, *NEAR)[:2]
    both = mm(jnp.concatenate([a1c[...], a1b[...]], axis=0), g_ref[0:128, :], NT)
    w_ref[0:192] = both[0:192]
    w_ref[192:288] = jnp.concatenate([both[192:288, 0:64], both[288:384, 0:64]], axis=1)
    bands_of = [
        mm(
            jnp.concatenate([x4[128 * s : 128 * s + 192, :], xh[32 * s : 32 * s + 48, :]], axis=0),
            h_ref[s],
            NT,
        )
        for s in range(2)
    ]
    r_ref[...] = bands_of[0][0:192] + bands_of[1][0:192]
    rh_ref[...] = bands_of[0][192:240] + bands_of[1][192:240]
    sums = tap_sums(r_ref, rh_ref)
    group = lax.shift_right_logical(lane_ids((12, LANES)), 5)
    w_ref[288:384] = jnp.zeros((96, LANES), F32)
    for k in range(3):
        packed = sums[4 * k]
        for n in range(1, 4):
            if 4 * k + n < 9:
                packed = jnp.where(group == n, sums[4 * k + n], packed)
        w_ref[288 + 16 * k : 300 + 16 * k] = packed
    zero = jnp.zeros((8, LANES), F32)
    for p in range(16):
        out_ref[p] = jnp.concatenate(
            [w_ref[p * PART : (p + 1) * PART], small[...], mix[p * 8 : (p + 1) * 8], zero], axis=0
        ).astype(BF)


def low_half(a, b):
    rows = lax.broadcasted_iota(jnp.int32, (8, LANES), 0)
    return jnp.where(rows < 4, a, pltpu.roll(b, 4, 0))


def high_half(a, b):
    rows = lax.broadcasted_iota(jnp.int32, (8, LANES), 0)
    return jnp.where(rows < 4, pltpu.roll(a, 4, 0), b)


def group_kernel(got, out_ref, d2_ref, d3_ref, loss_ref):
    even, odd = got[0].astype(F32), got[1].astype(F32)
    for k in range(1, 8):
        even, odd = even + got[2 * k].astype(F32), odd + got[2 * k + 1].astype(F32)
    total = even[0:PART] + odd[0:PART]
    d1 = low_half(even[32:40], odd[32:40])
    pay = jnp.concatenate([total, d1], axis=0).astype(BF)
    for k in range(16):
        out_ref[k] = pay
    d2_ref[...] = pltpu.roll(even[32:40], 4, 0)
    small = even[PART:32]
    d3_ref[...] = small[0:4, 0:64]
    lanes = lane_ids((8, LANES))
    rows = lax.broadcasted_iota(jnp.int32, (8, LANES), 0)
    held = jnp.logical_and(jnp.logical_and(lanes >= 64, lanes < 67), rows == 0)
    values = jnp.where(held, small, 0.0)
    loss_ref[...] = jnp.sum(jnp.sum(values, axis=1, keepdims=True), axis=0, keepdims=True)


def column_kernel(got, d2, out_ref):
    blocks = [got[k].astype(F32) for k in range(16)]
    total = blocks[0][0:PART]
    for b in blocks[1:]:
        total = total + b[0:PART]
    pay = jnp.concatenate([total, d2[...]] + [b[PART:32] for b in blocks], axis=0).astype(BF)
    for k in range(8):
        out_ref[k] = pay


def order_kernel(mine, out_ref, t_ref):
    for k in range(8):
        t_ref[k] = mine[k, 32:160].astype(F32)
        for r in range(4):
            out_ref[k, r * 32 : (r + 1) * 32] = t_ref[k, pl.ds(r, 32, stride=4), :]


def last_kernel(core, ordered, mine, other, gw1_ref, gw2_ref, gd1_ref, gd2_ref, w_ref, t_ref):
    first = core[0] == 0
    for k in range(8):
        at = pl.multiple_of(k * 256 + core[0] * 128, 128)
        gd1_ref[pl.ds(at, 128), :] = ordered[k]
        t_ref[k] = other[k, 32:160].astype(F32)
        base = k * 256 + (1 - core[0]) * 128
        for r in range(4):
            at = pl.multiple_of(base + r * 32, 32)
            gd1_ref[pl.ds(at, 32), :] = t_ref[k, pl.ds(r, 32, stride=4), :]
        a, b = mine[k, 0:32].astype(F32), other[k, 0:32].astype(F32)
        low, high = jnp.where(first, a, b), jnp.where(first, b, a)
        w_ref[2 * k * PART : (2 * k + 1) * PART] = low[0:PART]
        w_ref[(2 * k + 1) * PART : (2 * k + 2) * PART] = high[0:PART]
        gd2_ref[k * 8 : (k + 1) * 8] = low_half(low[PART:32], high[PART:32])
    for a in range(3):
        for e in range(3):
            gw2_ref[a, 0, e] = jnp.zeros((32, 64), F32)
            for b in (1, 2):
                at = e * 64 + (b - 1) * 32
                right = a == 0
                if a == 1:
                    right = at >= 96
                    at = 192 + at % 96
                block = w_ref[at : at + 32]
                if right:
                    block = pltpu.roll(block, 64, 1)
                gw2_ref[a, b, e] = block[:, 0:64]
    for a in range(3):
        for b in range(3):
            k, n = divmod(a * 3 + b, 4)
            packed = w_ref[288 + 16 * k : 304 + 16 * k]
            if n:
                packed = pltpu.roll(packed, LANES - 32 * n, 1)
            for e in range(3):
                gw1_ref[a, b, e] = packed[4 * e : 4 * e + 4, 0:32]


def local(volumes, targets, counts, w_conv1, w_conv2, w_dense1, w_dense2, w_dense3):
    core = lax.axis_index("core").astype(jnp.int32).reshape(1)
    position = lax.axis_index(SLABS).astype(jnp.int32).reshape(1)
    forward = [(i, i + 1) for i in range(31)]
    backward = [(i + 1, i) for i in range(31)]
    swap = [(0, 1), (1, 0)]
    split, own, rim = call(
        matrices_kernel,
        [((512, 640), BF), ((2, 2, 108, 192), BF), ((2, 108, 48), BF)],
        (),
        flops=2 * 10**9,
    )
    w1 = jnp.swapaxes(w_conv1, 3, 4).reshape(27, 4, 32)
    w2 = jnp.swapaxes(w_conv2, 3, 4)

    halo = lax.ppermute(volumes[:, :, 3], SLABS, forward)
    held_own, held_slope, away = call(
        first_kernel,
        [((sum(OWN), WIDE), BF), ((128, WIDE), BF), ((64, WIDE), BF)],
        (volumes, w1, w2, split, own),
        flops=10**9,
    )
    got = lax.ppermute(away, SLABS, forward)
    held_near, part, part_back = call(
        second_kernel,
        [((sum(NEAR), WIDE), BF), ((64, WIDE), F32), ((64, WIDE), BF)],
        (halo, split, w1, own, rim, w2, held_own, held_slope),
        flops=2 * 10**9,
    )
    part_next = lax.ppermute(part_back, SLABS, backward)
    slope2, pay, fown = call(
        third_kernel,
        [((64, WIDE), BF), ((32, 8, LANES), BF), ((S, LANES), BF)],
        (part, got),
        flops=3 * 10**9,
    )
    gathered = lax.all_to_all(pay, SLABS, 0, 0, tiled=True)
    next2, wd1, block = call(
        between_kernel,
        [((64, WIDE), BF), ((2048, LANES), BF), ((256, 256), BF)],
        (part_next, away, w_dense1, w2),
        scratch=[pltpu.VMEM((2048, LANES), F32)],
        flops=10**8,
    )
    gf, mix, small = call(
        tail_kernel,
        [((LANES, S), F32), ((LANES, LANES), F32), ((8, LANES), F32)],
        (gathered, wd1, w_dense2.T, w_dense3.T, targets.T, fown),
        scalars=(counts, position),
        scratch=[pltpu.VMEM((LANES, LANES), F32)],
        flops=2000000000,
    )
    (scattered,) = call(
        back_kernel,
        [((16, 48, LANES), BF)],
        (gf, mix, small, held_own, block, slope2, next2, held_near),
        scratch=[
            pltpu.VMEM((256, WIDE), BF), pltpu.VMEM((2, 128, WIDE), BF),
            pltpu.VMEM((16 * PART, LANES), F32), pltpu.VMEM((192, LANES), F32),
            pltpu.VMEM((48, LANES), F32),
        ],
        flops=2 * 10**9,
    )
    over_group = lax.all_to_all(scattered, (*DP, "core"), 0, 0, tiled=True)
    to_column, d2, d3, loss = call(
        group_kernel,
        [((16, 32, LANES), BF), ((8, LANES), F32), ((4, 64), F32), ((1, 1), F32)],
        (over_group,),
    )
    over_column = lax.all_to_all(to_column, COLUMN, 0, 0, tiled=True)
    (back,) = call(
        column_kernel, [((8, 160, LANES), BF)], (over_column, d2)
    )
    summed = lax.all_to_all(back, DP, 0, 0, tiled=True)
    other = lax.ppermute(summed, "core", swap)
    (ordered,) = call(
        order_kernel,
        [((8, LANES, LANES), F32)],
        (summed,),
        scratch=[pltpu.VMEM((8, LANES, LANES), F32)],
    )
    gw1, gw2, gd1, gd2 = call(
        last_kernel,
        [
            ((3, 3, 3, 4, 32), F32), ((3, 3, 3, 32, 64), F32),
            ((2048, LANES), F32), ((64, LANES), F32),
        ],
        (ordered, summed, other),
        scalars=(core,),
        scratch=[pltpu.VMEM((16 * PART, LANES), F32), pltpu.VMEM((8, LANES, LANES), F32)],
    )
    return (
        loss.reshape(()), jnp.swapaxes(gw1, 3, 4), jnp.swapaxes(gw2, 3, 4), gd1, gd2.T, d3.T,
    )


def solution(mesh):
    fine = Mesh(mesh.devices.reshape(4, 2, 2, 8, 2), ("x", "yl", "yh", "z", "core"))
    placed = (P(DP, None, SLABS, None, None), P(DP, None), P(), P(), P(), P(), P(), P())
    return jax.shard_map(
        local, mesh=fine, in_specs=placed, out_specs=(P(), P(), P(), P(), P(), P()), check_vma=False
    )
```
